512 devices in a mesh: seq: 8 (over x, core), head: 64 (over y, z).
Axes of the slice: x: 4, y: 4, z: 16, core: 2. Of those that a mesh axis runs over, the one named last changes fastest.
Arguments:
- q_rot: bfloat16 [8192, 8192], P(('seq', 'head')), may hold values from -4 to 4
- k_rot: bfloat16 [8192, 1024], P(('seq', 'head')), may hold values from -7 to 7
- v_rot: bfloat16 [8192, 1024], P(('seq', 'head')), may hold values from -6 to 6
- q_exp: int32 [512, 256], P(('seq', 'head')), may hold values from 0 to 1
- k_exp: int32 [512, 32], P(('seq', 'head')), may hold values from 0 to 1
- v_exp: int32 [512, 32], P(('seq', 'head')), may hold values from -1 to 1
- span_order: int32 [16], replicated, may hold values from 0 to 15, each once
- ffn_row: int32 [8, 1024], P('seq'), may hold values from 0 to 1023, each once within a row
Outputs:
- routed: bfloat16 [8192, 8192], P(('seq', 'head'))
The draws below stay inside these ranges and needn't reach their ends.
Inputs may be any that keep to these rules, and one draw needn't show every extreme that they name: `span_order`: each number of 0 to 15 once. Each row of ffn_row holds every number of 0 to 1023 once.
All inputs are finite; a program needn't handle non-finite values.
Results may differ from the reference program's by a relative error of at most 0.004.
Values may be sent and summed in bfloat16 or wider, within the bound.
No kernel may reach another device: no remote copies, remote signals or barrier semaphores. Data moves between devices by JAX's collectives and lax.ppermute only.
A program may use at most 64 MiB of HBM per device.

```python
import math
import jax
import jax.numpy as jnp
from jax import lax

HD = 128
GROUP = 8
HBLK = 32
QBLK = 16
HEADS = 64
KVH = 8
TOK_GRP = 1024
TOKENS = 8192
SPAN = 512
SPANS = 16
N_SEQ = 8


def draw_q_rot(key, part):
    key = jax.random.fold_in(key, 11)
    result = jnp.clip(jax.random.normal(key, (TOKENS, HEADS * HD), jnp.float32), -4.0, 4.0)
    return result.astype(jnp.bfloat16)


def draw_k_rot(key, part):
    key = jax.random.fold_in(key, 23)
    result = jnp.clip(jax.random.normal(key, (TOKENS, KVH * HD), jnp.float32), -4.0, 4.0)
    return result.astype(jnp.bfloat16)


def touch_ends(values, own_key, least, high):
    longest = values.shape.index(max(values.shape))
    spots = []
    for shift in (0, 1):
        where = [jax.random.randint(jax.random.fold_in(own_key, axis), (), 0, length) for axis, length in enumerate(values.shape)]
        where[longest] = (where[longest] + shift) % values.shape[longest]
        spots.append(tuple(where))
    return values.at[spots[0]].set(least).at[spots[1]].set(high)


def level_of(own_key, extent, pieces, smallest, high):
    gain, own = 1.0, jax.random.fold_in(own_key, 6)
    for axis_at, blocks in pieces:
        heights = jnp.exp(jax.random.uniform(jax.random.fold_in(own, axis_at), (blocks,), jnp.float32, smallest / len(pieces), high / len(pieces)))
        gain = gain * jnp.repeat(heights, extent[axis_at] // blocks).reshape([-1 if axis == axis_at else 1 for axis in range(len(extent))])
    return gain


def normal_values(rng, dims, scale, limit, cuts=(), kind=jnp.bfloat16):
    array = scale * jax.random.normal(rng, dims, jnp.float32)
    if cuts:
        array = array * level_of(rng, dims, cuts, -0.22, 0.18)
    return jnp.clip(array, -limit, limit).astype(kind)


def setup_inputs(seed: int = 0) -> dict:
    splits = jax.random.split(jax.random.key(seed), 9)
    return {
        "q_rot": draw_q_rot(jax.random.fold_in(splits[8], 71), 0),
        "k_rot": draw_k_rot(jax.random.fold_in(splits[8], 71), 0),
        "v_rot": normal_values(splits[2], (TOKENS, KVH * HD), 1.0, 6.0, ((0, 512),)),
        "q_exp": touch_ends(jax.random.randint(splits[3], (TOKENS // QBLK, HEADS * HD // HBLK), 0, 2), jax.random.fold_in(splits[3], 1), 0, 1).astype(jnp.int32),
        "k_exp": touch_ends(jax.random.randint(splits[4], (TOKENS // QBLK, KVH * HD // HBLK), 0, 2), jax.random.fold_in(splits[4], 1), 0, 1).astype(jnp.int32),
        "v_exp": touch_ends(jax.random.randint(splits[5], (TOKENS // QBLK, KVH * HD // HBLK), -1, 2), jax.random.fold_in(splits[5], 1), -1, 1).astype(jnp.int32),
        "span_order": jax.random.permutation(splits[6], SPANS).astype(jnp.int32),
        "ffn_row": jax.vmap(lambda own: jax.random.permutation(own, TOK_GRP))(jax.random.split(splits[7], N_SEQ)).reshape((N_SEQ, TOK_GRP)).astype(jnp.int32),
    }


NEG = -1e+30

def hadamard(size_n):
    idx = jnp.arange(size_n, dtype=jnp.int32)
    common_bits = idx[:, None] & idx[None, :]
    parity = jnp.zeros((size_n, size_n), jnp.int32)
    for bit_pos in range(size_n.bit_length() - 1):
        parity = parity + (common_bits >> bit_pos & 1)
    sign_table = 1.0 - 2.0 * (parity % 2).astype(jnp.float32)
    return sign_table / math.sqrt(size_n)

def dequantize(values_in, exponents):
    row_count, col_count = values_in.shape
    factor = jnp.exp2(exponents.astype(jnp.float32))
    shaped = values_in.astype(jnp.float32).reshape(row_count // QBLK, QBLK, col_count // HBLK, HBLK)
    return (shaped * factor[:, None, :, None]).reshape(row_count, col_count).astype(jnp.bfloat16)

def positions(row_ids, block_order, span_len):
    slot = row_ids // span_len
    slot_match = slot[:, None] == jnp.arange(block_order.shape[0], dtype=jnp.int32)[None, :]
    span_start = lax.optimization_barrier(jnp.sum(jnp.where(slot_match, block_order[None, :], 0), axis=1))
    return span_start * span_len + row_ids % span_len

def reference(q_rot, k_rot, v_rot, q_exp, k_exp, v_exp, span_order, ffn_row):
    query_deq = dequantize(q_rot, q_exp).reshape(TOKENS, HEADS, HD)
    key_deq = dequantize(k_rot, k_exp).reshape(TOKENS, KVH, HD)
    value_deq = dequantize(v_rot, v_exp).reshape(TOKENS, KVH, HD)
    row_ids = jnp.arange(TOKENS, dtype=jnp.int32)
    pos = positions(row_ids, span_order, SPAN)
    q_width = math.gcd(TOKENS, 1024)
    score_scale = 1.0 / math.sqrt(HD)

    def one_head(head_id):
        keys_f = lax.dynamic_index_in_dim(key_deq, head_id // GROUP, 1, keepdims=False).astype(jnp.float32)
        vals_b = lax.dynamic_index_in_dim(value_deq, head_id // GROUP, 1, keepdims=False)
        queries_f = lax.dynamic_index_in_dim(query_deq, head_id, 1, keepdims=False).astype(jnp.float32)

        def one_block(block_id):
            q_tile = lax.dynamic_slice_in_dim(queries_f, block_id * q_width, q_width, 0)
            q_pos = lax.dynamic_slice_in_dim(pos, block_id * q_width, q_width, 0)
            scores = jnp.dot(q_tile, keys_f.T, precision=lax.Precision.HIGHEST) * score_scale
            allowed = pos[None, :] <= q_pos[:, None]
            scores = jnp.where(allowed, scores, NEG)
            peak = lax.optimization_barrier(jnp.max(scores, axis=1))
            weights = jnp.where(allowed, jnp.exp(scores - peak[:, None]), 0.0)
            total = lax.optimization_barrier(jnp.sum(weights, axis=1))
            mixed = jnp.dot(weights.astype(jnp.bfloat16), vals_b, preferred_element_type=jnp.float32)
            return mixed / total[:, None]
        blocks = lax.map(one_block, jnp.arange(TOKENS // q_width, dtype=jnp.int32))
        return blocks.reshape(TOKENS, HD)
    attended = lax.map(one_head, jnp.arange(HEADS, dtype=jnp.int32))
    attended = jnp.transpose(attended, (1, 0, 2)).reshape(TOKENS, HEADS, HD // HBLK, HBLK)
    unrotated = jnp.einsum('rhbj,jk->rhbk', attended, hadamard(HBLK), precision=lax.Precision.HIGHEST)
    flat = unrotated.reshape(TOKENS, HEADS * HD).astype(jnp.bfloat16)
    ffn_dest = row_ids // TOK_GRP * TOK_GRP + ffn_row.reshape(TOKENS)
    return jnp.zeros((TOKENS, HEADS * HD), jnp.bfloat16).at[ffn_dest].set(flat)
```

```python
import functools
import math

import jax
import jax.numpy as jnp
from jax import lax
from jax.experimental import pallas as pl
from jax.experimental.pallas import tpu as pltpu
from jax.sharding import PartitionSpec as P

HD = 128
GROUP = 8
HBLK = 32
QBLK = 16
TILES = 4

NEG = -1e30
NT = (((1,), (1,)), ((), ()))
TN = (((0,), (0,)), ((), ()))


def dequantize(values_in, exponents):
    row_count, col_count = values_in.shape
    factor = jnp.exp2(exponents.astype(jnp.float32))
    shaped = values_in.astype(jnp.float32).reshape(row_count // QBLK, QBLK, col_count // HBLK, HBLK)
    return (shaped * factor[:, None, :, None]).reshape(row_count, col_count).astype(jnp.bfloat16)


def folded(tile):
    return jnp.sum(tile.reshape(tile.shape[0] // 8, 8, tile.shape[1]), axis=0)


def sign_table():
    i = lax.broadcasted_iota(jnp.int32, (HD, HD), 0)
    j = lax.broadcasted_iota(jnp.int32, (HD, HD), 1)
    both = i & j
    odd = (both ^ (both >> 1) ^ (both >> 2) ^ (both >> 3) ^ (both >> 4)) & 1
    return jnp.where(i // HBLK == j // HBLK, 1.0 - 2.0 * odd.astype(jnp.float32), 0.0).astype(jnp.bfloat16)


def attend_kernel(order_ref, group_ref, q_ref, k_ref, v_ref, row_ref, o_ref, slot_ref, peak, total, acc, flat, *, span):
    spans = order_ref.shape[0]
    rows = q_ref.shape[0]
    q_spans = rows // span
    rate = math.log2(math.e) / math.sqrt(HD)

    def note(stored, _):
        slot_ref[order_ref[stored]] = stored
        return 0

    lax.fori_loop(0, spans, note, 0)

    def span_of(ref, slot):
        return ref[pl.ds(pl.multiple_of(slot * span, span), span), :]

    for a in range(q_spans):
        q = q_ref[pl.ds(a * span, span), :]
        own = group_ref[0] * q_spans + a
        count = order_ref[own]

        def scores(slot):
            return lax.dot_general(span_of(k_ref, slot), q, NT, preferred_element_type=jnp.float32)

        def mixed(slot, weights):
            return lax.dot_general(
                span_of(v_ref, slot), weights.astype(jnp.bfloat16), TN, preferred_element_type=jnp.float32
            )

        key_at = lax.broadcasted_iota(jnp.int32, (span, span), 0)
        query_at = lax.broadcasted_iota(jnp.int32, (span, span), 1)
        first = jnp.where(key_at <= query_at, scores(own), NEG)
        top = jnp.max(first, axis=0, keepdims=True)
        weights = jnp.exp2((first - top) * rate)
        peak[...] = top
        total[...] = folded(weights)
        acc[...] = mixed(own, weights)

        def earlier(slots):
            tiles = [scores(slot) for slot in slots]
            old = peak[...]
            top = old
            for tile in tiles:
                top = jnp.maximum(top, jnp.max(tile, axis=0, keepdims=True))
            shrink = jnp.exp2((old - top) * rate)
            peak[...] = top
            summed = total[...] * shrink
            added = acc[...] * shrink
            for slot, tile in zip(slots, tiles):
                weights = jnp.exp2((tile - top) * rate)
                summed = summed + folded(weights)
                added = added + mixed(slot, weights)
            total[...] = summed
            acc[...] = added

        def step(t, _):
            earlier([slot_ref[TILES * t + i] for i in range(TILES)])
            return 0

        lax.fori_loop(0, count // TILES, step, 0)
        part = TILES // 2
        while part:
            @pl.when((count & part) != 0)
            def _(part=part):
                base = count & ~(2 * part - 1)
                earlier([slot_ref[base + i] for i in range(part)])

            part //= 2

        out = acc[...] * (1.0 / (jnp.sum(total[...], axis=0, keepdims=True) * math.sqrt(HBLK)))
        high = out.astype(jnp.bfloat16)
        low = (out - high.astype(jnp.float32)).astype(jnp.bfloat16)
        signs = sign_table()
        turned = jnp.dot(signs, high, preferred_element_type=jnp.float32)
        turned = turned + jnp.dot(signs, low, preferred_element_type=jnp.float32)
        flat[:, pl.ds(a * span, span)] = turned.astype(jnp.bfloat16)

    block = math.gcd(rows, 256)
    for start in range(0, rows, block):
        want = lax.broadcasted_iota(jnp.int32, (block, rows), 0) + start
        pick = jnp.where(row_ref[...] == want, 1.0, 0.0).astype(jnp.bfloat16)
        o_ref[pl.ds(start, block), :] = lax.dot_general(
            pick, flat[...], NT, preferred_element_type=jnp.float32
        ).astype(jnp.bfloat16)


def attend(order, group, q, k, v, row):
    rows = q.shape[0]
    span = k.shape[0] // order.shape[0]
    vmem = pl.BlockSpec(memory_space=pltpu.VMEM)
    smem = pl.BlockSpec(memory_space=pltpu.SMEM)
    return pl.pallas_call(
        functools.partial(attend_kernel, span=span),
        out_shape=jax.ShapeDtypeStruct((rows, HD), jnp.bfloat16),
        in_specs=[smem, smem, vmem, vmem, vmem, vmem],
        out_specs=vmem,
        scratch_shapes=[
            pltpu.SMEM((order.shape[0],), jnp.int32),
            pltpu.VMEM((1, span), jnp.float32),
            pltpu.VMEM((8, span), jnp.float32),
            pltpu.VMEM((HD, span), jnp.float32),
            pltpu.VMEM((HD, rows), jnp.bfloat16),
        ],
        compiler_params=pltpu.CompilerParams(vmem_limit_bytes=40 * 2**20),
        name="attend",
    )(order, group, q, k, v, row)


def widen(heads_in, row_count):
    shaped = heads_in.reshape(row_count, -1, HD)
    return jnp.repeat(shaped, GROUP, axis=1).reshape(row_count, -1)


def per_device(q_rot, k_rot, v_rot, q_exp, k_exp, v_exp, span_order, ffn_row):
    tok_dev = q_rot.shape[0]
    group = lax.axis_index("seq").astype(jnp.int32).reshape(1)
    query_deq = dequantize(q_rot, q_exp)
    key_deq = dequantize(k_rot, k_exp)
    value_deq = dequantize(v_rot, v_exp)
    head_q, head_k, head_v = (
        lax.all_to_all(query_deq, "head", split_axis=1, concat_axis=0, tiled=True),
        lax.all_to_all(widen(key_deq, tok_dev), "head", split_axis=1, concat_axis=0, tiled=True),
        lax.all_to_all(widen(value_deq, tok_dev), "head", split_axis=1, concat_axis=0, tiled=True),
    )
    piece_k = lax.all_gather(head_k, "seq", axis=0, tiled=True)
    piece_v = lax.all_gather(head_v, "seq", axis=0, tiled=True)
    placed = attend(span_order, group, head_q, piece_k, piece_v, ffn_row)
    return lax.all_to_all(placed, "head", split_axis=0, concat_axis=1, tiled=True)


def solution(mesh):
    return jax.shard_map(
        per_device,
        mesh=mesh,
        in_specs=(
            P(("seq", "head"), None),
            P(("seq", "head"), None),
            P(("seq", "head"), None),
            P(("seq", "head"), None),
            P(("seq", "head"), None),
            P(("seq", "head"), None),
            P(),
            P("seq", None),
        ),
        out_specs=P(("seq", "head"), None),
        check_vma=False,
    )
```

```python
import functools
import math

import jax
import jax.numpy as jnp
from jax import lax
from jax.experimental import pallas as pl
from jax.experimental.pallas import tpu as pltpu
from jax.sharding import Mesh, PartitionSpec as P

HD = 128
GROUP = 8
HBLK = 32
QBLK = 16
SPANS_GRP = 2
PARTS = 3
TAIL = 16

NEG = -1e30
NT = (((1,), (1,)), ((), ()))
TN = (((0,), (0,)), ((), ()))
PLANE = ("y", "kv", "pair")
NEAR = ("core", "y", "pair")


def dequantize(values_in, exponents):
    row_count, col_count = values_in.shape
    factor = jnp.exp2(exponents.astype(jnp.float32))
    shaped = values_in.astype(jnp.float32).reshape(row_count // QBLK, QBLK, col_count // HBLK, HBLK)
    return (shaped * factor[:, None, :, None]).reshape(row_count, col_count).astype(jnp.bfloat16)


def folded(tile):
    return jnp.sum(tile.reshape(tile.shape[0] // 8, 8, tile.shape[1]), axis=0)


def sign_table():
    i = lax.broadcasted_iota(jnp.int32, (HD, HD), 0)
    j = lax.broadcasted_iota(jnp.int32, (HD, HD), 1)
    both = i & j
    odd = (both ^ (both >> 1) ^ (both >> 2) ^ (both >> 3) ^ (both >> 4)) & 1
    return jnp.where(i // HBLK == j // HBLK, 1.0 - 2.0 * odd.astype(jnp.float32), 0.0).astype(jnp.bfloat16)


def partial_kernel(order_ref, place_ref, q_ref, kv_ref, o_ref, rank_ref, *, span):
    members = kv_ref.shape[0] // 2
    share = kv_ref.shape[1] // (2 * SPANS_GRP)
    per_member = share // (span // (members * 2))
    key_spans = 2 * SPANS_GRP
    first_key, target = place_ref[0] * SPANS_GRP, place_ref[1]
    rate = math.log2(math.e) / math.sqrt(HD)
    places = [order_ref[first_key + n] for n in range(key_spans)]
    for n in range(key_spans):
        rank = sum((places[m] < places[n]).astype(jnp.int32) for m in range(key_spans) if m != n)
        rank_ref[rank] = n

    def rows_of(n, half):
        at = half * (SPANS_GRP * share) + lax.rem(n, SPANS_GRP) * share
        tile = kv_ref[pl.ds(lax.div(n, SPANS_GRP) * members, members), pl.ds(pl.multiple_of(at, share), share), :]
        return tile.reshape(members * share, HD)

    for a in range(SPANS_GRP):
        at = pl.ds(a * span, span)
        q_place = order_ref[target * SPANS_GRP + a]
        count = sum((p <= q_place).astype(jnp.int32) for p in places)
        own = functools.reduce(jnp.logical_or, [p == q_place for p in places])

        def run(tiles, masked, at=at):
            q = q_ref[at, :]
            spans = [rank_ref[n] for n in range(tiles)]
            scored = [
                lax.dot_general(rows_of(n, 0), q, NT, preferred_element_type=jnp.float32) for n in spans
            ]
            if masked:
                r = lax.broadcasted_iota(jnp.int32, (span, span), 0)
                member, inside = r // share, r % share
                per_chunk = share // (span // QBLK)
                key_at = inside // per_chunk * QBLK + member * per_chunk + inside % per_chunk
                query_at = lax.broadcasted_iota(jnp.int32, (span, span), 1)
                scored[-1] = jnp.where(key_at <= query_at, scored[-1], NEG)
            top = functools.reduce(jnp.maximum, [jnp.max(s, axis=0, keepdims=True) for s in scored])
            total = jnp.zeros((8, span), jnp.float32)
            added = jnp.zeros((HD, span), jnp.float32)
            for n, s in zip(spans, scored):
                weights = jnp.exp2((s - top) * rate)
                total = total + folded(weights)
                added = added + lax.dot_general(
                    rows_of(n, 1), weights.astype(jnp.bfloat16), TN, preferred_element_type=jnp.float32
                )
            total = jnp.sum(total, axis=0, keepdims=True)
            put(added * (1.0 / total), top * rate + jnp.log2(total), at)

        def put(values, level, at):
            o_ref[0:HD, at] = values.astype(jnp.bfloat16)
            parts = []
            for _ in range(PARTS):
                part = level.astype(jnp.bfloat16)
                level = level - part.astype(jnp.float32)
                parts.append(part.astype(jnp.float32))
            row = lax.broadcasted_iota(jnp.int32, (TAIL, span), 0)
            tail = jnp.zeros((TAIL, span), jnp.float32)
            for n, part in enumerate(parts):
                tail = jnp.where(row == n, part, tail)
            o_ref[HD:HD + TAIL, at] = tail.astype(jnp.bfloat16)

        @pl.when(count == 0)
        def _(at=at, put=put):
            put(jnp.zeros((HD, span), jnp.float32), jnp.full((1, span), NEG, jnp.float32), at)

        for tiles in range(1, key_spans + 1):
            for masked in (False, True):
                @pl.when((count == tiles) & (own == masked))
                def _(run=run, tiles=tiles, masked=masked):
                    run(tiles, masked)


def attend_part(order, place, q, kv):
    rows = q.shape[0]
    span = rows // SPANS_GRP
    vmem = pl.BlockSpec(memory_space=pltpu.VMEM)
    smem = pl.BlockSpec(memory_space=pltpu.SMEM)
    keys = 2 * rows
    return pl.pallas_call(
        functools.partial(partial_kernel, span=span),
        out_shape=jax.ShapeDtypeStruct((HD + TAIL, rows), jnp.bfloat16),
        in_specs=[smem, smem, vmem, vmem],
        out_specs=vmem,
        scratch_shapes=[pltpu.SMEM((2 * SPANS_GRP,), jnp.int32)],
        compiler_params=pltpu.CompilerParams(vmem_limit_bytes=32 * 2**20),
        cost_estimate=pl.CostEstimate(
            flops=4 * rows * keys * HD, bytes_accessed=3 * 2**20, transcendentals=rows * keys
        ),
        name="attend_part",
    )(order, place, q, kv)


def merge_kernel(row_ref, *refs):
    parts, o_ref, flat = refs[:-2], refs[-2], refs[-1]
    rows = o_ref.shape[0]
    levels = []
    for ref in parts:
        tail = ref[HD:HD + TAIL, :].astype(jnp.float32)
        levels.append(jnp.sum(tail, axis=0, keepdims=True))
    top = functools.reduce(jnp.maximum, levels)
    shares = [jnp.exp2(level - top) for level in levels]
    whole = 1.0 / (sum(shares) * math.sqrt(HBLK))
    out = sum(ref[0:HD, :].astype(jnp.float32) * (share * whole) for ref, share in zip(parts, shares))
    high = out.astype(jnp.bfloat16)
    low = (out - high.astype(jnp.float32)).astype(jnp.bfloat16)
    signs = sign_table()
    turned = jnp.dot(signs, high, preferred_element_type=jnp.float32)
    turned = turned + jnp.dot(signs, low, preferred_element_type=jnp.float32)
    flat[...] = turned.astype(jnp.bfloat16)
    block = math.gcd(rows, 256)
    for start in range(0, rows, block):
        want = lax.broadcasted_iota(jnp.int32, (block, rows), 0) + start
        pick = jnp.where(row_ref[...] == want, 1.0, 0.0).astype(jnp.bfloat16)
        o_ref[pl.ds(start, block), :] = lax.dot_general(
            pick, flat[...], NT, preferred_element_type=jnp.float32
        ).astype(jnp.bfloat16)


def merge(row, parts):
    rows = row.shape[1]
    vmem = pl.BlockSpec(memory_space=pltpu.VMEM)
    return pl.pallas_call(
        merge_kernel,
        out_shape=jax.ShapeDtypeStruct((rows, HD), jnp.bfloat16),
        in_specs=[vmem] * (1 + len(parts)),
        out_specs=vmem,
        scratch_shapes=[pltpu.VMEM((HD, rows), jnp.bfloat16)],
        compiler_params=pltpu.CompilerParams(vmem_limit_bytes=32 * 2**20),
        cost_estimate=pl.CostEstimate(flops=2 * rows * rows * HD, bytes_accessed=2 * 2**20, transcendentals=0),
        name="merge",
    )(row, *parts)


def per_device(q_rot, k_rot, v_rot, q_exp, k_exp, v_exp, span_order, ffn_row):
    sizes = {name: lax.axis_size(name) for name in ("x", "core", "y", "kv", "pair")}
    n_x, n_core, n_y, n_kv, n_pair = sizes.values()
    x_at, core_at = lax.axis_index("x"), lax.axis_index("core")
    tok = q_rot.shape[0]
    share = tok // GROUP
    plane = n_y * n_kv * n_pair

    def to_plane(wide):
        return wide.reshape(tok, n_kv, n_y, n_pair, HD).transpose(2, 1, 3, 0, 4)

    def kv_share(narrow):
        shaped = narrow.reshape(n_y, n_pair, share, n_kv, HD)
        return shaped.transpose(0, 3, 1, 2, 4)

    query = to_plane(dequantize(q_rot, q_exp))
    key = kv_share(dequantize(k_rot, k_exp))
    value = kv_share(dequantize(v_rot, v_exp))
    message = jnp.concatenate([query, key, value], axis=3).reshape(plane, tok + 2 * share, HD)
    got = lax.all_to_all(message, PLANE, split_axis=0, concat_axis=0, tiled=True)
    q_own = got[:, :tok].reshape(plane * tok, HD)
    piece = jnp.concatenate(
        [got[:, tok:tok + share].reshape(plane * share, HD), got[:, tok + share:].reshape(plane * share, HD)], axis=0
    )

    def along_x(array, shift):
        return lax.ppermute(array, "x", [(i, (i + shift) % n_x) for i in range(n_x)])

    shifts = [n_x // 2] + [s for s in range(1, n_x) if s != n_x // 2]
    queries = {s: along_x(q_own, s) for s in shifts}
    near = n_core * n_y * n_pair
    kv = lax.all_to_all(
        jnp.broadcast_to(piece[None], (near,) + piece.shape), NEAR, split_axis=0, concat_axis=0, tiled=True
    )
    first_key = x_at * n_core
    results = []
    for s in shifts + [0]:
        source = lax.rem(x_at + n_x - s, n_x)
        place = jnp.stack([first_key, source * n_core + core_at]).astype(jnp.int32)
        done = attend_part(span_order, place, queries.get(s, q_own), kv)
        results.append(along_x(done, n_x - s) if s else done)
    placed = merge(ffn_row, results)
    back = lax.all_to_all(placed.reshape(plane, tok, HD), PLANE, split_axis=0, concat_axis=0, tiled=True)
    heads = back.reshape(n_y, n_kv, n_pair, tok, HD).transpose(3, 1, 0, 2, 4)
    return heads.reshape(tok, plane * HD)


def solution(mesh):
    devices = mesh.devices.reshape(4, 2, 4, 8, 2)
    axes = ("x", "core", "y", "kv", "pair")
    inner = Mesh(devices, axes)
    rows = P(axes, None)
    return jax.shard_map(
        per_device,
        mesh=inner,
        in_specs=(rows, rows, rows, rows, rows, rows, P(), P(("x", "core"), None)),
        out_specs=rows,
        check_vma=False,
    )
```

```python
import functools
import math

import jax
import jax.numpy as jnp
from jax import lax
from jax.experimental import pallas as pl
from jax.experimental.pallas import tpu as pltpu
from jax.sharding import Mesh, PartitionSpec as P

HD = 128
HBLK = 32
QBLK = 16
SPANS_GRP = 2
PARTS = 3
TAIL = 16
TILES = 2

NEG = -1e30
NT = (((1,), (1,)), ((), ()))
TN = (((0,), (0,)), ((), ()))
PLANE = ("y", "kv", "pair")
NEAR = ("core", "y")


def pack_kernel(q_ref, k_ref, v_ref, qe_ref, ke_ref, ve_ref, o_ref, *, n_y, n_kv, n_pair):
    tok = q_ref.shape[0]
    share = tok // n_y
    blocks = HD // HBLK
    spread = jnp.where(
        lax.broadcasted_iota(jnp.int32, (blocks, HD), 1) // HBLK == lax.broadcasted_iota(jnp.int32, (blocks, HD), 0),
        1.0,
        0.0,
    )

    def factors(ref):
        scale = jnp.exp2(ref[...].astype(jnp.float32))
        return sum(scale[:, b:b + 1] * spread[b:b + 1, :] for b in range(blocks))

    def head(ref, scale, n):
        return ref[:, n * HD:(n + 1) * HD].astype(jnp.float32) * scale[n:n + 1, :]

    q_scale, k_scale, v_scale = factors(qe_ref), factors(ke_ref), factors(ve_ref)
    for kv in range(n_kv):
        key, value = head(k_ref, k_scale, kv), head(v_ref, v_scale, kv)
        for y in range(n_y):
            at = slice(y * share, (y + 1) * share)
            for pair in range(n_pair):
                query = head(q_ref, q_scale, (kv * n_y + y) * n_pair + pair)
                rows = jnp.concatenate([query, key[at], value[at]], axis=0)
                o_ref[(y * n_kv + kv) * n_pair + pair] = rows.astype(jnp.bfloat16)


def pack(q_rot, k_rot, v_rot, q_exp, k_exp, v_exp, n_y, n_kv, n_pair):
    tok = q_rot.shape[0]
    vmem = pl.BlockSpec(memory_space=pltpu.VMEM)
    by_head = [e.reshape(-1, HD // HBLK) for e in (q_exp, k_exp, v_exp)]
    return pl.pallas_call(
        functools.partial(pack_kernel, n_y=n_y, n_kv=n_kv, n_pair=n_pair),
        out_shape=jax.ShapeDtypeStruct((n_y * n_kv * n_pair, tok + 2 * tok // n_y, HD), jnp.bfloat16),
        in_specs=[vmem] * 6,
        out_specs=vmem,
        compiler_params=pltpu.CompilerParams(vmem_limit_bytes=32 * 2**20),
        name="pack",
    )(q_rot, k_rot, v_rot, *by_head)


def folded(tile):
    return jnp.sum(tile.reshape(tile.shape[0] // 8, 8, tile.shape[1]), axis=0)


def sign_table():
    i = lax.broadcasted_iota(jnp.int32, (HD, HD), 0)
    j = lax.broadcasted_iota(jnp.int32, (HD, HD), 1)
    both = i & j
    odd = (both ^ (both >> 1) ^ (both >> 2) ^ (both >> 3) ^ (both >> 4)) & 1
    return jnp.where(i // HBLK == j // HBLK, 1.0 - 2.0 * odd.astype(jnp.float32), 0.0).astype(jnp.bfloat16)


def partial_kernel(order_ref, place_ref, kv_ref, *refs, span, targets):
    q_refs, o_refs = refs[:targets], refs[targets:2 * targets]
    rank_ref, q_ref, o_ref, scored, peak, total, acc = refs[2 * targets:]
    group = scored.shape[0] // span
    for n, ref in enumerate(q_refs):
        q_ref[n] = ref[...]
    members = kv_ref.shape[0] // 2
    share = kv_ref.shape[1] // (2 * SPANS_GRP)
    per_chunk = share * QBLK // span
    key_spans = 2 * SPANS_GRP
    first_key = place_ref[0] * SPANS_GRP
    rate = math.log2(math.e) / math.sqrt(HD)
    places = [order_ref[first_key + n] for n in range(key_spans)]
    for n in range(key_spans):
        rank = sum((places[m] < places[n]).astype(jnp.int32) for m in range(key_spans) if m != n)
        rank_ref[rank] = n

    def rows_of(n, half):
        at = half * (SPANS_GRP * share) + lax.rem(n, SPANS_GRP) * share
        tile = kv_ref[pl.ds(lax.div(n, SPANS_GRP) * members, members), pl.ds(pl.multiple_of(at, share), share), :]
        return tile.reshape(span, HD)

    def one(item, _):
        target = lax.div(item, SPANS_GRP)
        a = lax.rem(item, SPANS_GRP)
        q_place = order_ref[place_ref[1 + target] * SPANS_GRP + a]
        count = sum((p <= q_place).astype(jnp.int32) for p in places)
        own = functools.reduce(jnp.logical_or, [p == q_place for p in places])

        at = pl.ds(pl.multiple_of(a * span, span), span)
        q = q_ref[target, at, :]
        peak[...] = jnp.full_like(peak, NEG)
        total[...] = jnp.zeros_like(total)
        acc[...] = jnp.zeros_like(acc)

        def step(t, _):
            slots = [rank_ref[jnp.minimum(t * group + i, key_spans - 1)] for i in range(group)]
            for i, n in enumerate(slots):
                scored[pl.ds(i * span, span), :] = lax.dot_general(rows_of(n, 0), q, NT, preferred_element_type=jnp.float32)
            whole = count - t * group - own.astype(jnp.int32)

            def hide(r, _):
                rows = pl.ds(pl.multiple_of(r * share, share), share)
                inside = lax.broadcasted_iota(jnp.int32, (share, span), 0)
                key_at = inside // per_chunk * QBLK + lax.rem(r, members) * per_chunk + inside % per_chunk
                query_at = lax.broadcasted_iota(jnp.int32, (share, span), 1)
                on_edge = own & (lax.div(r, members) == whole)
                limit = jnp.where(on_edge, 0, -2 * span)
                scored[rows, :] = jnp.where(key_at <= query_at + limit, scored[rows, :], NEG)
                return 0

            lax.fori_loop(jnp.minimum(whole, group) * members, group * members, hide, 0)
            old = peak[...]
            top = old
            for i in range(group):
                top = jnp.maximum(top, jnp.max(scored[pl.ds(i * span, span), :], axis=0, keepdims=True))
            shrink = jnp.exp2((old - top) * rate)
            peak[...] = top
            summed = total[...] * shrink
            added = acc[...] * shrink
            for i, n in enumerate(slots):
                weights = jnp.exp2((scored[pl.ds(i * span, span), :] - top) * rate)
                summed = summed + folded(weights)
                added = added + lax.dot_general(rows_of(n, 1), weights.astype(jnp.bfloat16), TN, preferred_element_type=jnp.float32)
            total[...] = summed
            acc[...] = added
            return 0

        lax.fori_loop(0, lax.div(count + group - 1, group), step, 0)
        summed = jnp.sum(total[...], axis=0, keepdims=True)
        some = summed > 0.0
        safe = jnp.where(some, summed, 1.0)
        o_ref[target, 0:HD, at] = (acc[...] * (1.0 / safe)).astype(jnp.bfloat16)
        level = jnp.where(some, peak[...] * rate + jnp.log2(safe), NEG)
        row = lax.broadcasted_iota(jnp.int32, (TAIL, span), 0)
        tail = jnp.zeros((TAIL, span), jnp.float32)
        for n in range(PARTS):
            part = level.astype(jnp.bfloat16).astype(jnp.float32)
            level = level - part
            tail = jnp.where(row == n, part, tail)
        o_ref[target, HD:HD + TAIL, at] = tail.astype(jnp.bfloat16)
        return 0

    lax.fori_loop(0, targets * SPANS_GRP, one, 0)
    for n, ref in enumerate(o_refs):
        ref[...] = o_ref[n]


def attend_part(order, place, queries, kv):
    targets, rows = len(queries), queries[0].shape[0]
    span = rows // SPANS_GRP
    vmem = pl.BlockSpec(memory_space=pltpu.VMEM)
    smem = pl.BlockSpec(memory_space=pltpu.SMEM)
    keys = 2 * rows
    one = jax.ShapeDtypeStruct((HD + TAIL, rows), jnp.bfloat16)
    return pl.pallas_call(
        functools.partial(partial_kernel, span=span, targets=targets),
        out_shape=[one] * targets,
        in_specs=[smem, smem] + [vmem] * (1 + targets),
        out_specs=[vmem] * targets,
        scratch_shapes=[
            pltpu.SMEM((2 * SPANS_GRP,), jnp.int32),
            pltpu.VMEM((targets, rows, HD), jnp.bfloat16),
            pltpu.VMEM((targets, HD + TAIL, rows), jnp.bfloat16),
            pltpu.VMEM((TILES * span, span), jnp.float32),
            pltpu.VMEM((1, span), jnp.float32),
            pltpu.VMEM((8, span), jnp.float32),
            pltpu.VMEM((HD, span), jnp.float32),
        ],
        compiler_params=pltpu.CompilerParams(vmem_limit_bytes=32 * 2**20),
        cost_estimate=pl.CostEstimate(
            flops=4 * targets * rows * keys * HD, bytes_accessed=3 * 2**20, transcendentals=targets * rows * keys
        ),
        name="attend_part",
    )(order, place, kv, *queries)


def merge_kernel(row_ref, *refs):
    parts, o_ref, flat = refs[:-2], refs[-2], refs[-1]
    rows = o_ref.shape[0]
    levels = []
    for ref in parts:
        tail = ref[HD:HD + TAIL, :].astype(jnp.float32)
        levels.append(jnp.sum(tail, axis=0, keepdims=True))
    top = functools.reduce(jnp.maximum, levels)
    shares = [jnp.exp2(level - top) for level in levels]
    whole = 1.0 / (sum(shares) * math.sqrt(HBLK))
    out = sum(ref[0:HD, :].astype(jnp.float32) * (share * whole) for ref, share in zip(parts, shares))
    high = out.astype(jnp.bfloat16)
    low = (out - high.astype(jnp.float32)).astype(jnp.bfloat16)
    signs = sign_table()
    turned = jnp.dot(signs, high, preferred_element_type=jnp.float32)
    turned = turned + jnp.dot(signs, low, preferred_element_type=jnp.float32)
    flat[...] = turned.astype(jnp.bfloat16)
    block = math.gcd(rows, 256)
    for start in range(0, rows, block):
        want = lax.broadcasted_iota(jnp.int32, (block, rows), 0) + start
        pick = jnp.where(row_ref[...] == want, 1.0, 0.0).astype(jnp.bfloat16)
        o_ref[pl.ds(start, block), :] = lax.dot_general(
            pick, flat[...], NT, preferred_element_type=jnp.float32
        ).astype(jnp.bfloat16)


def merge(row, parts):
    rows = row.shape[1]
    vmem = pl.BlockSpec(memory_space=pltpu.VMEM)
    return pl.pallas_call(
        merge_kernel,
        out_shape=jax.ShapeDtypeStruct((rows, HD), jnp.bfloat16),
        in_specs=[vmem] * (1 + len(parts)),
        out_specs=vmem,
        scratch_shapes=[pltpu.VMEM((HD, rows), jnp.bfloat16)],
        compiler_params=pltpu.CompilerParams(vmem_limit_bytes=32 * 2**20),
        cost_estimate=pl.CostEstimate(flops=2 * rows * rows * HD, bytes_accessed=2 * 2**20, transcendentals=0),
        name="merge",
    )(row, *parts)


def per_device(q_rot, k_rot, v_rot, q_exp, k_exp, v_exp, span_order, ffn_row):
    sizes = {name: lax.axis_size(name) for name in ("x", "core", "y", "kv", "pair")}
    n_x, n_core, n_y, n_kv, n_pair = sizes.values()
    x_at, core_at = lax.axis_index("x"), lax.axis_index("core")
    tok = q_rot.shape[0]
    share = tok // n_y
    plane = n_y * n_kv * n_pair
    message = pack(q_rot, k_rot, v_rot, q_exp, k_exp, v_exp, n_y, n_kv, n_pair)
    got = lax.all_to_all(message, PLANE, split_axis=0, concat_axis=0, tiled=True)
    q_own = got[:, :tok].reshape(plane * tok, HD)
    piece = jnp.concatenate(
        [got[:, tok:tok + share].reshape(plane * share, HD), got[:, tok + share:].reshape(plane * share, HD)], axis=0
    )

    def along_x(array, shift):
        return lax.ppermute(array, "x", [(i, (i + shift) % n_x) for i in range(n_x)])

    shifts = [n_x // 2] + [s for s in range(1, n_x) if s != n_x // 2]
    queries = [along_x(q_own, s) for s in shifts]
    near = n_core * n_y
    kv = lax.all_to_all(
        jnp.broadcast_to(piece[None], (near,) + piece.shape), NEAR, split_axis=0, concat_axis=0, tiled=True
    )

    def place(moves):
        groups = [lax.rem(x_at + n_x - s, n_x) * n_core + core_at for s in moves]
        return jnp.stack([x_at * n_core] + groups).astype(jnp.int32)

    others = attend_part(span_order, place(shifts), queries, kv)
    results = [along_x(part, n_x - s) for part, s in zip(others, shifts)]
    results += attend_part(span_order, place([0]), [q_own], kv)
    placed = merge(ffn_row, results)
    back = lax.all_to_all(placed.reshape(plane, tok, HD), PLANE, split_axis=0, concat_axis=0, tiled=True)
    heads = back.reshape(n_y, n_kv, n_pair, tok, HD).transpose(3, 1, 0, 2, 4)
    return heads.reshape(tok, plane * HD)


def solution(mesh):
    devices = mesh.devices.reshape(4, 2, 4, 8, 2)
    axes = ("x", "core", "y", "kv", "pair")
    inner = Mesh(devices, axes)
    rows = P(axes, None)
    return jax.shard_map(
        per_device,
        mesh=inner,
        in_specs=(rows, rows, rows, rows, rows, rows, P(), P(("x", "core"), None)),
        out_specs=rows,
        check_vma=False,
    )
```

```python
import functools
import math

import jax
import jax.numpy as jnp
from jax import lax
from jax.experimental import pallas as pl
from jax.experimental.pallas import tpu as pltpu
from jax.sharding import Mesh, PartitionSpec as P

HD = 128
HBLK = 32
QBLK = 16
SPANS_GRP = 2
PARTS = 3
TAIL = 16
TILES = 2

NEG = -1e30
NT = (((1,), (1,)), ((), ()))
TN = (((0,), (0,)), ((), ()))
PLANE = ("y", "kv", "pair")
NEAR = ("core", "y")


def factors(ref):
    width = ref.shape[1]
    blocks = HD // HBLK
    heads = width // blocks
    scale = jnp.exp2(ref[...].astype(jnp.float32))
    head = lax.broadcasted_iota(jnp.int32, (heads, width), 0)
    at = lax.broadcasted_iota(jnp.int32, (heads, width), 1)
    picked = jnp.where(at // blocks == head, scale, 0.0).astype(jnp.bfloat16)
    at = lax.broadcasted_iota(jnp.int32, (width, HD), 0)
    lane = lax.broadcasted_iota(jnp.int32, (width, HD), 1)
    spread = jnp.where(at % blocks == lane // HBLK, 1.0, 0.0).astype(jnp.bfloat16)
    return jnp.dot(picked, spread, preferred_element_type=jnp.float32)


def pack_kernel(*refs, n_y, n_kv, n_pair):
    count = 6
    sources, o_ref, held, sems = refs[:count], refs[count], refs[count + 1:2 * count + 1], refs[2 * count + 1]
    copies = [pltpu.make_async_copy(src, dst, sems.at[n]) for n, (src, dst) in enumerate(zip(sources, held))]
    for copy in copies:
        copy.start()
    for copy in copies:
        copy.wait()
    q_ref, k_ref, v_ref, qe_ref, ke_ref, ve_ref = held
    share = q_ref.shape[0] // n_y

    def head(ref, scale, n):
        return ref[:, n * HD:(n + 1) * HD].astype(jnp.float32) * scale[n:n + 1, :]

    q_scale, k_scale, v_scale = factors(qe_ref), factors(ke_ref), factors(ve_ref)
    for kv in range(n_kv):
        key, value = head(k_ref, k_scale, kv), head(v_ref, v_scale, kv)
        for y in range(n_y):
            at = slice(y * share, (y + 1) * share)
            for pair in range(n_pair):
                query = head(q_ref, q_scale, (kv * n_y + y) * n_pair + pair)
                rows = jnp.concatenate([query, key[at], value[at]], axis=0)
                o_ref[(y * n_kv + kv) * n_pair + pair] = rows.astype(jnp.bfloat16)


def pack(arrays, n_y, n_kv, n_pair):
    tok = arrays[0].shape[0]
    return pl.pallas_call(
        functools.partial(pack_kernel, n_y=n_y, n_kv=n_kv, n_pair=n_pair),
        out_shape=jax.ShapeDtypeStruct((n_y * n_kv * n_pair, tok + 2 * tok // n_y, HD), jnp.bfloat16),
        in_specs=[pl.BlockSpec(memory_space=pl.ANY)] * len(arrays),
        out_specs=pl.BlockSpec(memory_space=pltpu.VMEM),
        scratch_shapes=[pltpu.VMEM(a.shape, a.dtype) for a in arrays] + [pltpu.SemaphoreType.DMA((len(arrays),))],
        compiler_params=pltpu.CompilerParams(vmem_limit_bytes=60 * 2**20),
        name="pack",
    )(*arrays)


def folded(tile):
    return jnp.sum(tile.reshape(tile.shape[0] // 8, 8, tile.shape[1]), axis=0)


def sign_table():
    i = lax.broadcasted_iota(jnp.int32, (HD, HD), 0)
    j = lax.broadcasted_iota(jnp.int32, (HD, HD), 1)
    both = i & j
    odd = (both ^ (both >> 1) ^ (both >> 2) ^ (both >> 3) ^ (both >> 4)) & 1
    return jnp.where(i // HBLK == j // HBLK, 1.0 - 2.0 * odd.astype(jnp.float32), 0.0).astype(jnp.bfloat16)


def partial_kernel(order_ref, place_ref, kv_ref, *refs, span, targets):
    q_refs, o_refs = refs[:targets], refs[targets:2 * targets]
    rank_ref, q_ref, o_ref, scored, peak, total, acc = refs[2 * targets:]
    group = scored.shape[0] // span
    for n, ref in enumerate(q_refs):
        q_ref[n] = ref[...]
    members = kv_ref.shape[0] // 2
    share = kv_ref.shape[1] // (2 * SPANS_GRP)
    per_chunk = share * QBLK // span
    key_spans = 2 * SPANS_GRP
    first_key = place_ref[0] * SPANS_GRP
    rate = math.log2(math.e) / math.sqrt(HD)
    places = [order_ref[first_key + n] for n in range(key_spans)]
    for n in range(key_spans):
        rank = sum((places[m] < places[n]).astype(jnp.int32) for m in range(key_spans) if m != n)
        rank_ref[rank] = n

    def rows_of(n, half):
        at = half * (SPANS_GRP * share) + lax.rem(n, SPANS_GRP) * share
        tile = kv_ref[pl.ds(lax.div(n, SPANS_GRP) * members, members), pl.ds(pl.multiple_of(at, share), share), :]
        return tile.reshape(span, HD)

    def one(item, _):
        target = lax.div(item, SPANS_GRP)
        a = lax.rem(item, SPANS_GRP)
        q_place = order_ref[place_ref[1 + target] * SPANS_GRP + a]
        count = sum((p <= q_place).astype(jnp.int32) for p in places)
        own = functools.reduce(jnp.logical_or, [p == q_place for p in places])

        at = pl.ds(pl.multiple_of(a * span, span), span)
        q = q_ref[target, at, :]
        peak[...] = jnp.full_like(peak, NEG)
        total[...] = jnp.zeros_like(total)
        acc[...] = jnp.zeros_like(acc)

        def step(t, _):
            slots = [rank_ref[jnp.minimum(t * group + i, key_spans - 1)] for i in range(group)]
            for i, n in enumerate(slots):
                scored[pl.ds(i * span, span), :] = lax.dot_general(rows_of(n, 0), q, NT, preferred_element_type=jnp.float32)
            whole = count - t * group - own.astype(jnp.int32)

            def hide(r, _):
                rows = pl.ds(pl.multiple_of(r * share, share), share)
                inside = lax.broadcasted_iota(jnp.int32, (share, span), 0)
                key_at = inside // per_chunk * QBLK + lax.rem(r, members) * per_chunk + inside % per_chunk
                query_at = lax.broadcasted_iota(jnp.int32, (share, span), 1)
                on_edge = own & (lax.div(r, members) == whole)
                limit = jnp.where(on_edge, 0, -2 * span)
                scored[rows, :] = jnp.where(key_at <= query_at + limit, scored[rows, :], NEG)
                return 0

            lax.fori_loop(jnp.minimum(whole, group) * members, group * members, hide, 0)
            old = peak[...]
            top = old
            for i in range(group):
                top = jnp.maximum(top, jnp.max(scored[pl.ds(i * span, span), :], axis=0, keepdims=True))
            shrink = jnp.exp2((old - top) * rate)
            peak[...] = top
            summed = total[...] * shrink
            added = acc[...] * shrink
            for i, n in enumerate(slots):
                weights = jnp.exp2((scored[pl.ds(i * span, span), :] - top) * rate)
                summed = summed + folded(weights)
                added = added + lax.dot_general(rows_of(n, 1), weights.astype(jnp.bfloat16), TN, preferred_element_type=jnp.float32)
            total[...] = summed
            acc[...] = added
            return 0

        lax.fori_loop(0, lax.div(count + group - 1, group), step, 0)
        summed = jnp.sum(total[...], axis=0, keepdims=True)
        some = summed > 0.0
        safe = jnp.where(some, summed, 1.0)
        o_ref[target, 0:HD, at] = (acc[...] * (1.0 / safe)).astype(jnp.bfloat16)
        level = jnp.where(some, peak[...] * rate + jnp.log2(safe), NEG)
        row = lax.broadcasted_iota(jnp.int32, (TAIL, span), 0)
        tail = jnp.zeros((TAIL, span), jnp.float32)
        for n in range(PARTS):
            part = level.astype(jnp.bfloat16).astype(jnp.float32)
            level = level - part
            tail = jnp.where(row == n, part, tail)
        o_ref[target, HD:HD + TAIL, at] = tail.astype(jnp.bfloat16)
        return 0

    lax.fori_loop(0, targets * SPANS_GRP, one, 0)
    for n, ref in enumerate(o_refs):
        ref[...] = o_ref[n]


def attend_part(order, place, queries, kv):
    targets, rows = len(queries), queries[0].shape[0]
    span = rows // SPANS_GRP
    vmem = pl.BlockSpec(memory_space=pltpu.VMEM)
    smem = pl.BlockSpec(memory_space=pltpu.SMEM)
    keys = 2 * rows
    one = jax.ShapeDtypeStruct((HD + TAIL, rows), jnp.bfloat16)
    return pl.pallas_call(
        functools.partial(partial_kernel, span=span, targets=targets),
        out_shape=[one] * targets,
        in_specs=[smem, smem] + [vmem] * (1 + targets),
        out_specs=[vmem] * targets,
        scratch_shapes=[
            pltpu.SMEM((2 * SPANS_GRP,), jnp.int32),
            pltpu.VMEM((targets, rows, HD), jnp.bfloat16),
            pltpu.VMEM((targets, HD + TAIL, rows), jnp.bfloat16),
            pltpu.VMEM((TILES * span, span), jnp.float32),
            pltpu.VMEM((1, span), jnp.float32),
            pltpu.VMEM((8, span), jnp.float32),
            pltpu.VMEM((HD, span), jnp.float32),
        ],
        compiler_params=pltpu.CompilerParams(vmem_limit_bytes=32 * 2**20),
        cost_estimate=pl.CostEstimate(
            flops=4 * targets * rows * keys * HD, bytes_accessed=3 * 2**20, transcendentals=targets * rows * keys
        ),
        name="attend_part",
    )(order, place, kv, *queries)


def merge_kernel(row_ref, *refs):
    parts, o_ref, flat = refs[:-2], refs[-2], refs[-1]
    rows = o_ref.shape[0]
    levels = []
    for ref in parts:
        tail = ref[HD:HD + TAIL, :].astype(jnp.float32)
        levels.append(jnp.sum(tail, axis=0, keepdims=True))
    top = functools.reduce(jnp.maximum, levels)
    shares = [jnp.exp2(level - top) for level in levels]
    whole = 1.0 / (sum(shares) * math.sqrt(HBLK))
    out = sum(ref[0:HD, :].astype(jnp.float32) * (share * whole) for ref, share in zip(parts, shares))
    high = out.astype(jnp.bfloat16)
    low = (out - high.astype(jnp.float32)).astype(jnp.bfloat16)
    signs = sign_table()
    turned = jnp.dot(signs, high, preferred_element_type=jnp.float32)
    turned = turned + jnp.dot(signs, low, preferred_element_type=jnp.float32)
    flat[...] = turned.astype(jnp.bfloat16)
    block = math.gcd(rows, 256)
    for start in range(0, rows, block):
        want = lax.broadcasted_iota(jnp.int32, (block, rows), 0) + start
        pick = jnp.where(row_ref[...] == want, 1.0, 0.0).astype(jnp.bfloat16)
        o_ref[pl.ds(start, block), :] = lax.dot_general(
            pick, flat[...], NT, preferred_element_type=jnp.float32
        ).astype(jnp.bfloat16)


def merge(row, parts):
    rows = row.shape[1]
    vmem = pl.BlockSpec(memory_space=pltpu.VMEM)
    return pl.pallas_call(
        merge_kernel,
        out_shape=jax.ShapeDtypeStruct((rows, HD), jnp.bfloat16),
        in_specs=[vmem] * (1 + len(parts)),
        out_specs=vmem,
        scratch_shapes=[pltpu.VMEM((HD, rows), jnp.bfloat16)],
        compiler_params=pltpu.CompilerParams(vmem_limit_bytes=32 * 2**20),
        cost_estimate=pl.CostEstimate(flops=2 * rows * rows * HD, bytes_accessed=2 * 2**20, transcendentals=0),
        name="merge",
    )(row, *parts)


def per_device(q_rot, k_rot, v_rot, q_exp, k_exp, v_exp, span_order, ffn_row):
    sizes = {name: lax.axis_size(name) for name in ("x", "core", "y", "kv", "pair")}
    n_x, n_core, n_y, n_kv, n_pair = sizes.values()
    x_at, core_at = lax.axis_index("x"), lax.axis_index("core")
    tok = q_rot.shape[0]
    share = tok // n_y
    plane = n_y * n_kv * n_pair
    message = pack((q_rot, k_rot, v_rot, q_exp, k_exp, v_exp), n_y, n_kv, n_pair)
    got = lax.all_to_all(message, PLANE, split_axis=0, concat_axis=0, tiled=True)
    q_own = got[:, :tok].reshape(plane * tok, HD)
    piece = got[:, tok:].reshape(plane, 2, share, HD).transpose(1, 0, 2, 3).reshape(2 * plane * share, HD)

    def along_x(array, shift):
        return lax.ppermute(array, "x", [(i, (i + shift) % n_x) for i in range(n_x)])

    shifts = [n_x // 2] + [s for s in range(1, n_x) if s != n_x // 2]
    queries = [along_x(q_own, s) for s in shifts]
    near = n_core * n_y
    kv = lax.all_to_all(
        jnp.broadcast_to(piece[None], (near,) + piece.shape), NEAR, split_axis=0, concat_axis=0, tiled=True
    )

    def place(moves):
        groups = [lax.rem(x_at + n_x - s, n_x) * n_core + core_at for s in moves]
        return jnp.stack([x_at * n_core] + groups).astype(jnp.int32)

    far, near_by = shifts[:1], shifts[1:]
    first = attend_part(span_order, place(far), queries[:1], kv)
    results = [along_x(part, n_x - s) for part, s in zip(first, far)]
    others = attend_part(span_order, place(near_by), queries[1:], kv)
    results += [along_x(part, n_x - s) for part, s in zip(others, near_by)]
    results += attend_part(span_order, place([0]), [q_own], kv)
    placed = merge(ffn_row, results)
    back = lax.all_to_all(placed.reshape(plane, tok, HD), PLANE, split_axis=0, concat_axis=0, tiled=True)
    heads = back.reshape(n_y, n_kv, n_pair, tok, HD).transpose(3, 1, 0, 2, 4)
    return heads.reshape(tok, plane * HD)


def solution(mesh):
    devices = mesh.devices.reshape(4, 2, 4, 8, 2)
    axes = ("x", "core", "y", "kv", "pair")
    inner = Mesh(devices, axes)
    rows = P(axes, None)
    return jax.shard_map(
        per_device,
        mesh=inner,
        in_specs=(rows, rows, rows, rows, rows, rows, P(), P(("x", "core"), None)),
        out_specs=rows,
        check_vma=False,
    )
```

```python
import functools
import math

import jax
import jax.numpy as jnp
from jax import lax
from jax.experimental import pallas as pl
from jax.experimental.pallas import tpu as pltpu
from jax.sharding import Mesh, PartitionSpec as P

HD = 128
HBLK = 32
QBLK = 16
SPANS_GRP = 2
PARTS = 3
TAIL = 16
LOW, HIGH = 2.0**-80, 2.0**110

NEG = -1e30
NT = (((1,), (1,)), ((), ()))
TN = (((0,), (0,)), ((), ()))
PLANE = ("y", "kv", "pair")
ROW = ("xh", "xl")
NEAR = ("xl", "y")


def factors(ref):
    width = ref.shape[1]
    blocks = HD // HBLK
    heads = width // blocks
    scale = jnp.exp2(ref[...].astype(jnp.float32))
    head = lax.broadcasted_iota(jnp.int32, (heads, width), 0)
    at = lax.broadcasted_iota(jnp.int32, (heads, width), 1)
    picked = jnp.where(at // blocks == head, scale, 0.0).astype(jnp.bfloat16)
    at = lax.broadcasted_iota(jnp.int32, (width, HD), 0)
    lane = lax.broadcasted_iota(jnp.int32, (width, HD), 1)
    spread = jnp.where(at % blocks == lane // HBLK, 1.0, 0.0).astype(jnp.bfloat16)
    return jnp.dot(picked, spread, preferred_element_type=jnp.float32)


def pack_kernel(*refs, n_y, n_kv, n_pair):
    count = 6
    sources, o_ref, held, sems = refs[:count], refs[count], refs[count + 1:2 * count + 1], refs[2 * count + 1]
    copies = [pltpu.make_async_copy(src, dst, sems.at[n]) for n, (src, dst) in enumerate(zip(sources, held))]
    for copy in copies:
        copy.start()
    for copy in copies:
        copy.wait()
    q_ref, k_ref, v_ref, qe_ref, ke_ref, ve_ref = held
    share = q_ref.shape[0] // n_y

    def head(ref, scale, n):
        return ref[:, n * HD:(n + 1) * HD].astype(jnp.float32) * scale[n:n + 1, :]

    q_scale, k_scale, v_scale = factors(qe_ref), factors(ke_ref), factors(ve_ref)
    for kv in range(n_kv):
        key, value = head(k_ref, k_scale, kv), head(v_ref, v_scale, kv)
        for y in range(n_y):
            at = slice(y * share, (y + 1) * share)
            for pair in range(n_pair):
                query = head(q_ref, q_scale, (kv * n_y + y) * n_pair + pair)
                rows = jnp.concatenate([query, key[at], value[at]], axis=0)
                o_ref[(y * n_kv + kv) * n_pair + pair] = rows.astype(jnp.bfloat16)


def pack(arrays, n_y, n_kv, n_pair):
    tok = arrays[0].shape[0]
    return pl.pallas_call(
        functools.partial(pack_kernel, n_y=n_y, n_kv=n_kv, n_pair=n_pair),
        out_shape=jax.ShapeDtypeStruct((n_y * n_kv * n_pair, tok + 2 * tok // n_y, HD), jnp.bfloat16),
        in_specs=[pl.BlockSpec(memory_space=pl.ANY)] * len(arrays),
        out_specs=pl.BlockSpec(memory_space=pltpu.VMEM),
        scratch_shapes=[pltpu.VMEM(a.shape, a.dtype) for a in arrays] + [pltpu.SemaphoreType.DMA((len(arrays),))],
        compiler_params=pltpu.CompilerParams(vmem_limit_bytes=60 * 2**20),
        name="pack",
    )(*arrays)


def folded(tile):
    return jnp.sum(tile.reshape(tile.shape[0] // 8, 8, tile.shape[1]), axis=0)


def sign_table():
    i = lax.broadcasted_iota(jnp.int32, (HD, HD), 0)
    j = lax.broadcasted_iota(jnp.int32, (HD, HD), 1)
    both = i & j
    odd = (both ^ (both >> 1) ^ (both >> 2) ^ (both >> 3) ^ (both >> 4)) & 1
    return jnp.where(i // HBLK == j // HBLK, 1.0 - 2.0 * odd.astype(jnp.float32), 0.0).astype(jnp.bfloat16)


def partial_kernel(order_ref, place_ref, *refs, span, targets, groups, edge):
    kv_refs, q_refs, o_refs = refs[:2], refs[2:2 + targets], refs[2 + targets:2 + 2 * targets]
    q_ref, o_ref, key, value, least, most, scored, peak, total, acc = refs[2 + 2 * targets:]
    members = 2 * kv_refs[0].shape[0] // groups
    share = kv_refs[0].shape[1] // (2 * SPANS_GRP)
    per_chunk = share * QBLK // span
    key_spans = groups * SPANS_GRP
    rate = math.log2(math.e) / math.sqrt(HD)
    places = [order_ref[place_ref[n // SPANS_GRP] * SPANS_GRP + n % SPANS_GRP] for n in range(key_spans)]

    for n, ref in enumerate(q_refs):
        q_ref[n] = ref[...]
    for n in range(key_spans):
        rank = sum((places[m] < places[n]).astype(jnp.int32) for m in range(key_spans) if m != n)
        at = pl.ds(pl.multiple_of(rank * span, span), span)
        for half, ref in enumerate((key, value)):
            kv_ref, group = kv_refs[n // (key_spans // 2)], n // SPANS_GRP % (groups // 2)
            start = (half * SPANS_GRP + n % SPANS_GRP) * share
            rows = kv_ref[pl.ds(group * members, members), pl.ds(start, share), :]
            ref[at, :] = rows.reshape(span, HD)
    least[...] = jnp.ones_like(least)
    most[...] = jnp.ones_like(most)

    def shown(s, q_index):
        inside = lax.broadcasted_iota(jnp.int32, s.shape, 0)
        chunk = inside % share
        key_at = chunk // per_chunk * QBLK + inside // share * per_chunk + chunk % per_chunk
        return key_at <= lax.broadcasted_iota(jnp.int32, s.shape, 1) + q_index

    def write(target, at, summed, level):
        o_ref[target, 0:HD, at] = (acc[...] * (1.0 / summed)).astype(jnp.bfloat16)
        row = lax.broadcasted_iota(jnp.int32, (TAIL, span), 0)
        tail = jnp.zeros((TAIL, span), jnp.float32)
        for n in range(PARTS):
            part = level.astype(jnp.bfloat16).astype(jnp.float32)
            level = level - part
            tail = jnp.where(row == n, part, tail)
        o_ref[target, HD:HD + TAIL, at] = tail.astype(jnp.bfloat16)

    def sight(item):
        target = lax.div(item, SPANS_GRP)
        a = lax.rem(item, SPANS_GRP)
        q_place = order_ref[place_ref[groups + target] * SPANS_GRP + a]
        count = sum((p <= q_place).astype(jnp.int32) for p in places)
        own = functools.reduce(jnp.logical_or, [p == q_place for p in places])
        at = pl.ds(pl.multiple_of(a * span, span), span)
        return target, at, count, count - own.astype(jnp.int32)

    def one(item, _):
        target, at, count, whole = sight(item)
        q = q_ref[target, at, :]
        total[...] = jnp.zeros_like(total)
        acc[...] = jnp.zeros_like(acc)

        def add(start, width, masked):
            rows = pl.ds(pl.multiple_of(start * span, span), width * span)
            s = lax.dot_general(key[rows, :], q, NT, preferred_element_type=jnp.float32) * rate
            if masked:
                s = jnp.where(shown(s, jnp.where(start < whole, span, 0)), s, NEG)
            weights = jnp.exp2(s)
            total[...] += folded(weights)
            acc[...] += lax.dot_general(
                value[rows, :], weights.astype(jnp.bfloat16), TN, preferred_element_type=jnp.float32
            )

        def two(t, _):
            add(2 * t, 2, False)
            return 0

        def single(t, _):
            add(t, 1, edge)
            return 0

        pairs = lax.div(whole, 2)
        lax.fori_loop(0, pairs, two, 0)
        lax.fori_loop(2 * pairs, count, single, 0)
        summed = jnp.sum(total[...], axis=0, keepdims=True)
        summed = jnp.where(count > 0, summed, 1.0)
        least[...] = jnp.minimum(least[...], summed)
        most[...] = jnp.maximum(most[...], summed)
        write(target, at, summed, jnp.where(count > 0, jnp.log2(summed), NEG))
        return 0

    lax.fori_loop(0, targets * SPANS_GRP, one, 0)

    def again(item, _):
        target, at, count, whole = sight(item)
        q = q_ref[target, at, :]
        peak[...] = jnp.full_like(peak, NEG)
        total[...] = jnp.zeros_like(total)
        acc[...] = jnp.zeros_like(acc)

        def step(t, _):
            rows = pl.ds(pl.multiple_of(t * span, span), span)
            s = lax.dot_general(key[rows, :], q, NT, preferred_element_type=jnp.float32)
            scored[...] = jnp.where(shown(s, jnp.where(t < whole, span, 0)), s, NEG)
            old = peak[...]
            top = jnp.maximum(old, jnp.max(scored[...], axis=0, keepdims=True))
            shrink = jnp.exp2((old - top) * rate)
            weights = jnp.exp2((scored[...] - top) * rate)
            peak[...] = top
            total[...] = total[...] * shrink + folded(weights)
            acc[...] = acc[...] * shrink + lax.dot_general(
                value[rows, :], weights.astype(jnp.bfloat16), TN, preferred_element_type=jnp.float32
            )
            return 0

        lax.fori_loop(0, count, step, 0)
        summed = jnp.sum(total[...], axis=0, keepdims=True)
        summed = jnp.where(count > 0, summed, 1.0)
        write(target, at, summed, jnp.where(count > 0, peak[...] * rate + jnp.log2(summed), NEG))
        return 0

    safe = (jnp.min(least[...]) > LOW) & (jnp.max(most[...]) < HIGH)

    @pl.when(jnp.logical_not(safe))
    def _():
        lax.fori_loop(0, targets * SPANS_GRP, again, 0)

    for n, ref in enumerate(o_refs):
        ref[...] = o_ref[n]


def attend_part(order, place, queries, kv, edge):
    targets, rows = len(queries), queries[0].shape[0]
    span = rows // SPANS_GRP
    vmem = pl.BlockSpec(memory_space=pltpu.VMEM)
    smem = pl.BlockSpec(memory_space=pltpu.SMEM)
    groups = sum(part.shape[0] * part.shape[1] for part in kv) // (2 * rows)
    keys = groups * rows
    one = jax.ShapeDtypeStruct((HD + TAIL, rows), jnp.bfloat16)
    return pl.pallas_call(
        functools.partial(partial_kernel, span=span, targets=targets, groups=groups, edge=edge),
        out_shape=[one] * targets,
        in_specs=[smem, smem] + [vmem] * (2 + targets),
        out_specs=[vmem] * targets,
        scratch_shapes=[
            pltpu.VMEM((targets, rows, HD), jnp.bfloat16),
            pltpu.VMEM((targets, HD + TAIL, rows), jnp.bfloat16),
            pltpu.VMEM((keys, HD), jnp.bfloat16),
            pltpu.VMEM((keys, HD), jnp.bfloat16),
            pltpu.VMEM((1, span), jnp.float32),
            pltpu.VMEM((1, span), jnp.float32),
            pltpu.VMEM((span, span), jnp.float32),
            pltpu.VMEM((1, span), jnp.float32),
            pltpu.VMEM((8, span), jnp.float32),
            pltpu.VMEM((HD, span), jnp.float32),
        ],
        compiler_params=pltpu.CompilerParams(vmem_limit_bytes=32 * 2**20),
        cost_estimate=pl.CostEstimate(
            flops=4 * targets * rows * keys * HD, bytes_accessed=3 * 2**20, transcendentals=targets * rows * keys
        ),
        name="attend_part",
    )(order, place, *kv, *queries)


def merge_kernel(row_ref, *refs):
    parts, o_ref, flat = refs[:-2], refs[-2], refs[-1]
    rows = o_ref.shape[0]
    levels = []
    for ref in parts:
        tail = ref[HD:HD + TAIL, :].astype(jnp.float32)
        levels.append(jnp.sum(tail, axis=0, keepdims=True))
    top = functools.reduce(jnp.maximum, levels)
    shares = [jnp.exp2(level - top) for level in levels]
    whole = 1.0 / (sum(shares) * math.sqrt(HBLK))
    out = sum(ref[0:HD, :].astype(jnp.float32) * (share * whole) for ref, share in zip(parts, shares))
    high = out.astype(jnp.bfloat16)
    low = (out - high.astype(jnp.float32)).astype(jnp.bfloat16)
    signs = sign_table()
    turned = jnp.dot(signs, high, preferred_element_type=jnp.float32)
    turned = turned + jnp.dot(signs, low, preferred_element_type=jnp.float32)
    flat[...] = turned.astype(jnp.bfloat16)
    block = math.gcd(rows, 256)
    for start in range(0, rows, block):
        want = lax.broadcasted_iota(jnp.int32, (block, rows), 0) + start
        pick = jnp.where(row_ref[...] == want, 1.0, 0.0).astype(jnp.bfloat16)
        o_ref[pl.ds(start, block), :] = lax.dot_general(
            pick, flat[...], NT, preferred_element_type=jnp.float32
        ).astype(jnp.bfloat16)


def merge(row, parts):
    rows = row.shape[1]
    vmem = pl.BlockSpec(memory_space=pltpu.VMEM)
    return pl.pallas_call(
        merge_kernel,
        out_shape=jax.ShapeDtypeStruct((rows, HD), jnp.bfloat16),
        in_specs=[vmem] * (1 + len(parts)),
        out_specs=vmem,
        scratch_shapes=[pltpu.VMEM((HD, rows), jnp.bfloat16)],
        compiler_params=pltpu.CompilerParams(vmem_limit_bytes=32 * 2**20),
        cost_estimate=pl.CostEstimate(flops=2 * rows * rows * HD, bytes_accessed=2 * 2**20, transcendentals=0),
        name="merge",
    )(row, *parts)


def per_device(q_rot, k_rot, v_rot, q_exp, k_exp, v_exp, span_order, ffn_row):
    n_xl, n_y, n_kv, n_pair = (lax.axis_size(name) for name in ("xl", "y", "kv", "pair"))
    n_x, n_core = lax.axis_size(ROW), lax.axis_size("core")
    x_at, core_at = lax.axis_index(ROW), lax.axis_index("core")
    tok = q_rot.shape[0]
    share = tok // n_y
    plane = n_y * n_kv * n_pair
    message = pack((q_rot, k_rot, v_rot, q_exp, k_exp, v_exp), n_y, n_kv, n_pair)
    got = lax.all_to_all(message, PLANE, split_axis=0, concat_axis=0, tiled=True)
    q_own = got[:, :tok].reshape(plane * tok, HD)
    piece = got[:, tok:].reshape(plane, 2, share, HD).transpose(1, 0, 2, 3).reshape(2 * plane * share, HD)

    def across(array):
        return lax.ppermute(array, ROW, [(i, n_x - 1 - i) for i in range(n_x)])

    q_far = across(q_own)
    near = n_xl * n_y
    kv = lax.all_to_all(
        jnp.broadcast_to(piece[None], (near,) + piece.shape), NEAR, split_axis=0, concat_axis=0, tiled=True
    )
    kv, q_far = lax.optimization_barrier((kv, q_far))
    kv = (kv, lax.ppermute(kv, "core", [(0, 1), (1, 0)]))
    first = lax.div(x_at, n_xl) * n_xl
    held = [(first + i) * n_core + c for c in (core_at, 1 - core_at) for i in range(n_xl)]

    def place(x):
        return jnp.stack(held + [x * n_core + core_at]).astype(jnp.int32)

    far, = attend_part(span_order, place(n_x - 1 - x_at), [q_far], kv, False)
    own, = attend_part(span_order, place(x_at), [q_own], kv, True)
    results = [across(far), own]
    placed = merge(ffn_row, results)
    back = lax.all_to_all(placed.reshape(plane, tok, HD), PLANE, split_axis=0, concat_axis=0, tiled=True)
    heads = back.reshape(n_y, n_kv, n_pair, tok, HD).transpose(3, 1, 0, 2, 4)
    return heads.reshape(tok, plane * HD)


def solution(mesh):
    devices = mesh.devices.reshape(2, 2, 2, 4, 8, 2)
    axes = ("xh", "xl", "core", "y", "kv", "pair")
    inner = Mesh(devices, axes)
    rows = P(axes, None)
    return jax.shard_map(
        per_device,
        mesh=inner,
        in_specs=(rows, rows, rows, rows, rows, rows, P(), P(("xh", "xl", "core"), None)),
        out_specs=rows,
        check_vma=False,
    )
```

```python
import functools
import math

import jax
import jax.numpy as jnp
from jax import lax
from jax.experimental import pallas as pl
from jax.experimental.pallas import tpu as pltpu
from jax.sharding import Mesh, PartitionSpec as P

HD = 128
HBLK = 32
QBLK = 16
SPANS_GRP = 2
PARTS = 3
TAIL = 16
ONES = 8
LOW, HIGH = 2.0**-80, 2.0**110

NEG = -1e30
NT = (((1,), (1,)), ((), ()))
TN = (((0,), (0,)), ((), ()))
PLANE = ("y", "kv", "pair")
ROW = ("xh", "xl")
NEAR = ("xl", "y")


def factors(ref):
    width = ref.shape[1]
    blocks = HD // HBLK
    heads = width // blocks
    scale = jnp.exp2(ref[...].astype(jnp.float32))
    head = lax.broadcasted_iota(jnp.int32, (heads, width), 0)
    at = lax.broadcasted_iota(jnp.int32, (heads, width), 1)
    picked = jnp.where(at // blocks == head, scale, 0.0).astype(jnp.bfloat16)
    at = lax.broadcasted_iota(jnp.int32, (width, HD), 0)
    lane = lax.broadcasted_iota(jnp.int32, (width, HD), 1)
    spread = jnp.where(at % blocks == lane // HBLK, 1.0, 0.0).astype(jnp.bfloat16)
    return jnp.dot(picked, spread, preferred_element_type=jnp.float32)


def pack_kernel(*refs, n_y, n_kv, n_pair):
    count = 6
    sources, o_ref, held, sems = refs[:count], refs[count], refs[count + 1:2 * count + 1], refs[2 * count + 1]
    copies = [pltpu.make_async_copy(src, dst, sems.at[n]) for n, (src, dst) in enumerate(zip(sources, held))]
    for copy in copies:
        copy.start()
    for copy in copies:
        copy.wait()
    q_ref, k_ref, v_ref, qe_ref, ke_ref, ve_ref = held
    share = q_ref.shape[0] // n_y

    def head(ref, scale, n):
        return ref[:, n * HD:(n + 1) * HD].astype(jnp.float32) * scale[n:n + 1, :]

    q_scale, k_scale, v_scale = factors(qe_ref), factors(ke_ref), factors(ve_ref)
    for kv in range(n_kv):
        key, value = head(k_ref, k_scale, kv), head(v_ref, v_scale, kv)
        for y in range(n_y):
            at = slice(y * share, (y + 1) * share)
            for pair in range(n_pair):
                query = head(q_ref, q_scale, (kv * n_y + y) * n_pair + pair)
                rows = jnp.concatenate([query, key[at], value[at]], axis=0)
                o_ref[(y * n_kv + kv) * n_pair + pair] = rows.astype(jnp.bfloat16)


def pack(arrays, n_y, n_kv, n_pair):
    tok = arrays[0].shape[0]
    return pl.pallas_call(
        functools.partial(pack_kernel, n_y=n_y, n_kv=n_kv, n_pair=n_pair),
        out_shape=jax.ShapeDtypeStruct((n_y * n_kv * n_pair, tok + 2 * tok // n_y, HD), jnp.bfloat16),
        in_specs=[pl.BlockSpec(memory_space=pl.ANY)] * len(arrays),
        out_specs=pl.BlockSpec(memory_space=pltpu.VMEM),
        scratch_shapes=[pltpu.VMEM(a.shape, a.dtype) for a in arrays] + [pltpu.SemaphoreType.DMA((len(arrays),))],
        compiler_params=pltpu.CompilerParams(vmem_limit_bytes=60 * 2**20),
        name="pack",
    )(*arrays)


def folded(tile):
    return jnp.sum(tile.reshape(tile.shape[0] // 8, 8, tile.shape[1]), axis=0)


def sign_table():
    i = lax.broadcasted_iota(jnp.int32, (HD, HD), 0)
    j = lax.broadcasted_iota(jnp.int32, (HD, HD), 1)
    both = i & j
    odd = (both ^ (both >> 1) ^ (both >> 2) ^ (both >> 3) ^ (both >> 4)) & 1
    return jnp.where(i // HBLK == j // HBLK, 1.0 - 2.0 * odd.astype(jnp.float32), 0.0).astype(jnp.bfloat16)


def partial_kernel(order_ref, place_ref, near_ref, other_ref, q_ref, o_ref, key, value, least, most, scored, peak, acc, *, span, groups, edge):
    kv_refs = (near_ref, other_ref)
    members = 2 * kv_refs[0].shape[0] // groups
    share = kv_refs[0].shape[1] // (2 * SPANS_GRP)
    per_chunk = share * QBLK // span
    key_spans = groups * SPANS_GRP
    rate = math.log2(math.e) / math.sqrt(HD)
    places = [order_ref[place_ref[n // SPANS_GRP] * SPANS_GRP + n % SPANS_GRP] for n in range(key_spans)]

    for n in range(key_spans):
        rank = sum((places[m] < places[n]).astype(jnp.int32) for m in range(key_spans) if m != n)
        at = pl.ds(pl.multiple_of(rank * span, span), span)
        for half, ref in enumerate((key, value)):
            kv_ref, group = kv_refs[n // (key_spans // 2)], n // SPANS_GRP % (groups // 2)
            start = (half * SPANS_GRP + n % SPANS_GRP) * share
            rows = kv_ref[pl.ds(group * members, members), pl.ds(start, share), :]
            ref[at, 0:HD] = rows.reshape(span, HD)
    value[:, HD:HD + ONES] = jnp.ones((value.shape[0], ONES), value.dtype)
    least[...] = jnp.ones_like(least)
    most[...] = jnp.ones_like(most)

    def shown(s, q_index):
        inside = lax.broadcasted_iota(jnp.int32, s.shape, 0)
        chunk = inside % share
        key_at = chunk // per_chunk * QBLK + inside // share * per_chunk + chunk % per_chunk
        return key_at <= lax.broadcasted_iota(jnp.int32, s.shape, 1) + q_index

    def write(at, summed, level):
        o_ref[0:HD, at] = (acc[0:HD, :] * (1.0 / summed)).astype(o_ref.dtype)
        row = lax.broadcasted_iota(jnp.int32, (TAIL, span), 0)
        tail = jnp.zeros((TAIL, span), jnp.float32)
        for n in range(PARTS):
            part = level.astype(jnp.bfloat16).astype(jnp.float32)
            level = level - part
            tail = jnp.where(row == n, part, tail)
        o_ref[HD:HD + TAIL, at] = tail.astype(o_ref.dtype)

    def sight(a):
        q_place = order_ref[place_ref[groups] * SPANS_GRP + a]
        count = sum((p <= q_place).astype(jnp.int32) for p in places)
        own = functools.reduce(jnp.logical_or, [p == q_place for p in places])
        at = pl.ds(pl.multiple_of(a * span, span), span)
        return at, count, count - own.astype(jnp.int32)

    def one(a, _):
        at, count, whole = sight(a)
        q = q_ref[at, :]
        acc[...] = jnp.zeros_like(acc)

        def add(start, width, masked):
            rows = pl.ds(pl.multiple_of(start * span, span), width * span)
            s = lax.dot_general(key[rows, :], q, NT, preferred_element_type=jnp.float32) * rate
            if masked:
                s = jnp.where(shown(s, jnp.where(start < whole, span, 0)), s, NEG)
            weights = jnp.exp2(s).astype(jnp.bfloat16)
            acc[...] += lax.dot_general(value[rows, :], weights, TN, preferred_element_type=jnp.float32)

        def two(t, _):
            add(2 * t, 2, False)
            return 0

        def single(t, _):
            add(t, 1, edge)
            return 0

        pairs = lax.div(whole, 2)
        lax.fori_loop(0, pairs, two, 0)
        lax.fori_loop(2 * pairs, count, single, 0)
        summed = acc[HD:HD + 1, :]
        summed = jnp.where(count > 0, summed, 1.0)
        least[...] = jnp.minimum(least[...], summed)
        most[...] = jnp.maximum(most[...], summed)
        write(at, summed, jnp.where(count > 0, jnp.log2(summed), NEG))
        return 0

    lax.fori_loop(0, SPANS_GRP, one, 0)

    def again(a, _):
        at, count, whole = sight(a)
        q = q_ref[at, :]
        peak[...] = jnp.full_like(peak, NEG)
        acc[...] = jnp.zeros_like(acc)

        def step(t, _):
            rows = pl.ds(pl.multiple_of(t * span, span), span)
            s = lax.dot_general(key[rows, :], q, NT, preferred_element_type=jnp.float32)
            scored[...] = jnp.where(shown(s, jnp.where(t < whole, span, 0)), s, NEG)
            old = peak[...]
            top = jnp.maximum(old, jnp.max(scored[...], axis=0, keepdims=True))
            shrink = jnp.exp2((old - top) * rate)
            weights = jnp.exp2((scored[...] - top) * rate)
            peak[...] = top
            acc[...] = acc[...] * shrink + lax.dot_general(
                value[rows, :], weights.astype(jnp.bfloat16), TN, preferred_element_type=jnp.float32
            )
            return 0

        lax.fori_loop(0, count, step, 0)
        summed = acc[HD:HD + 1, :]
        summed = jnp.where(count > 0, summed, 1.0)
        write(at, summed, jnp.where(count > 0, peak[...] * rate + jnp.log2(summed), NEG))
        return 0

    safe = (jnp.min(least[...]) > LOW) & (jnp.max(most[...]) < HIGH)

    @pl.when(jnp.logical_not(safe))
    def _():
        lax.fori_loop(0, SPANS_GRP, again, 0)


def attend_part(order, place, query, kv, edge, dtype):
    rows = query.shape[0]
    span = rows // SPANS_GRP
    vmem = pl.BlockSpec(memory_space=pltpu.VMEM)
    smem = pl.BlockSpec(memory_space=pltpu.SMEM)
    groups = sum(part.shape[0] * part.shape[1] for part in kv) // (2 * rows)
    keys = groups * rows
    return pl.pallas_call(
        functools.partial(partial_kernel, span=span, groups=groups, edge=edge),
        out_shape=jax.ShapeDtypeStruct((HD + TAIL, rows), dtype),
        in_specs=[smem, smem] + [vmem] * 3,
        out_specs=vmem,
        scratch_shapes=[
            pltpu.VMEM((keys, HD), jnp.bfloat16),
            pltpu.VMEM((keys, HD + ONES), jnp.bfloat16),
            pltpu.VMEM((1, span), jnp.float32),
            pltpu.VMEM((1, span), jnp.float32),
            pltpu.VMEM((span, span), jnp.float32),
            pltpu.VMEM((1, span), jnp.float32),
            pltpu.VMEM((HD + ONES, span), jnp.float32),
        ],
        compiler_params=pltpu.CompilerParams(vmem_limit_bytes=32 * 2**20),
        cost_estimate=pl.CostEstimate(
            flops=4 * rows * keys * HD, bytes_accessed=3 * 2**20, transcendentals=rows * keys
        ),
        name="attend_part",
    )(order, place, *kv, query)


def merge_kernel(row_ref, *refs):
    parts, o_ref, flat = refs[:-2], refs[-2], refs[-1]
    rows = o_ref.shape[0]
    levels = []
    for ref in parts:
        tail = ref[HD:HD + TAIL, :].astype(jnp.float32)
        levels.append(jnp.sum(tail, axis=0, keepdims=True))
    top = functools.reduce(jnp.maximum, levels)
    shares = [jnp.exp2(level - top) for level in levels]
    whole = 1.0 / (sum(shares) * math.sqrt(HBLK))
    out = sum(ref[0:HD, :].astype(jnp.float32) * (share * whole) for ref, share in zip(parts, shares))
    high = out.astype(jnp.bfloat16)
    low = (out - high.astype(jnp.float32)).astype(jnp.bfloat16)
    signs = sign_table()
    turned = jnp.dot(signs, high, preferred_element_type=jnp.float32)
    turned = turned + jnp.dot(signs, low, preferred_element_type=jnp.float32)
    flat[...] = turned.astype(jnp.bfloat16)
    block = math.gcd(rows, 256)
    for start in range(0, rows, block):
        want = lax.broadcasted_iota(jnp.int32, (block, rows), 0) + start
        pick = jnp.where(row_ref[...] == want, 1.0, 0.0).astype(jnp.bfloat16)
        o_ref[pl.ds(start, block), :] = lax.dot_general(
            pick, flat[...], NT, preferred_element_type=jnp.float32
        ).astype(jnp.bfloat16)


def merge(row, parts):
    rows = row.shape[1]
    vmem = pl.BlockSpec(memory_space=pltpu.VMEM)
    return pl.pallas_call(
        merge_kernel,
        out_shape=jax.ShapeDtypeStruct((rows, HD), jnp.bfloat16),
        in_specs=[vmem] * (1 + len(parts)),
        out_specs=vmem,
        scratch_shapes=[pltpu.VMEM((HD, rows), jnp.bfloat16)],
        compiler_params=pltpu.CompilerParams(vmem_limit_bytes=32 * 2**20),
        cost_estimate=pl.CostEstimate(flops=2 * rows * rows * HD, bytes_accessed=2 * 2**20, transcendentals=0),
        name="merge",
    )(row, *parts)


def per_device(q_rot, k_rot, v_rot, q_exp, k_exp, v_exp, span_order, ffn_row):
    n_xl, n_y, n_kv, n_pair = (lax.axis_size(name) for name in ("xl", "y", "kv", "pair"))
    n_x, n_core = lax.axis_size(ROW), lax.axis_size("core")
    x_at, core_at = lax.axis_index(ROW), lax.axis_index("core")
    tok = q_rot.shape[0]
    share = tok // n_y
    plane = n_y * n_kv * n_pair
    message = pack((q_rot, k_rot, v_rot, q_exp, k_exp, v_exp), n_y, n_kv, n_pair)
    got = lax.all_to_all(message, PLANE, split_axis=0, concat_axis=0, tiled=True)
    q_own = got[:, :tok].reshape(plane * tok, HD)
    piece = got[:, tok:].reshape(plane, 2, share, HD).transpose(1, 0, 2, 3).reshape(2 * plane * share, HD)

    def across(array):
        return lax.ppermute(array, ROW, [(i, n_x - 1 - i) for i in range(n_x)])

    q_far = across(q_own)
    near = n_xl * n_y
    kv = lax.all_to_all(
        jnp.broadcast_to(piece[None], (near,) + piece.shape), NEAR, split_axis=0, concat_axis=0, tiled=True
    )
    kv, q_far = lax.optimization_barrier((kv, q_far))
    kv = (kv, lax.ppermute(kv, "core", [(0, 1), (1, 0)]))
    first = lax.div(x_at, n_xl) * n_xl
    held = [(first + i) * n_core + c for c in (core_at, 1 - core_at) for i in range(n_xl)]

    def place(x):
        return jnp.stack(held + [x * n_core + core_at]).astype(jnp.int32)

    far = attend_part(span_order, place(n_x - 1 - x_at), q_far, kv, False, jnp.bfloat16)
    own = attend_part(span_order, place(x_at), q_own, kv, True, jnp.float32)
    results = [across(far), own]
    placed = merge(ffn_row, results)
    back = lax.all_to_all(placed.reshape(plane, tok, HD), PLANE, split_axis=0, concat_axis=0, tiled=True)
    heads = back.reshape(n_y, n_kv, n_pair, tok, HD).transpose(3, 1, 0, 2, 4)
    return heads.reshape(tok, plane * HD)


def solution(mesh):
    devices = mesh.devices.reshape(2, 2, 2, 4, 8, 2)
    axes = ("xh", "xl", "core", "y", "kv", "pair")
    inner = Mesh(devices, axes)
    rows = P(axes, None)
    return jax.shard_map(
        per_device,
        mesh=inner,
        in_specs=(rows, rows, rows, rows, rows, rows, P(), P(("xh", "xl", "core"), None)),
        out_specs=rows,
        check_vma=False,
    )
```

```python
import functools
import math

import jax
import jax.numpy as jnp
from jax import lax
from jax.experimental import pallas as pl
from jax.experimental.pallas import tpu as pltpu
from jax.sharding import Mesh, PartitionSpec as P

HD = 128
HBLK = 32
QBLK = 16
SPANS_GRP = 2
PARTS = 3
TAIL = 16
ONES = 8
LOW, HIGH = 2.0**-80, 2.0**110

NEG = -1e30
NT = (((1,), (1,)), ((), ()))
TN = (((0,), (0,)), ((), ()))
PLANE = ("y", "kv", "pair")
ROW = ("xh", "xl")
NEAR = ("xl", "y")


def factors(ref):
    width = ref.shape[1]
    blocks = HD // HBLK
    heads = width // blocks
    scale = jnp.exp2(ref[...].astype(jnp.float32))
    head = lax.broadcasted_iota(jnp.int32, (heads, width), 0)
    at = lax.broadcasted_iota(jnp.int32, (heads, width), 1)
    picked = jnp.where(at // blocks == head, scale, 0.0).astype(jnp.bfloat16)
    at = lax.broadcasted_iota(jnp.int32, (width, HD), 0)
    lane = lax.broadcasted_iota(jnp.int32, (width, HD), 1)
    spread = jnp.where(at % blocks == lane // HBLK, 1.0, 0.0).astype(jnp.bfloat16)
    return jnp.dot(picked, spread, preferred_element_type=jnp.float32)


def pack_kernel(*refs, n_y, n_kv, n_pair):
    count = 6
    sources, o_ref, held, sems = refs[:count], refs[count], refs[count + 1:2 * count + 1], refs[2 * count + 1]
    copies = [pltpu.make_async_copy(src, dst, sems.at[n]) for n, (src, dst) in enumerate(zip(sources, held))]
    for copy in copies:
        copy.start()
    for copy in copies:
        copy.wait()
    q_ref, k_ref, v_ref, qe_ref, ke_ref, ve_ref = held
    share = q_ref.shape[0] // n_y

    def head(ref, scale, n):
        return ref[:, n * HD:(n + 1) * HD].astype(jnp.float32) * scale[n:n + 1, :]

    q_scale, k_scale, v_scale = factors(qe_ref), factors(ke_ref), factors(ve_ref)
    for kv in range(n_kv):
        key, value = head(k_ref, k_scale, kv), head(v_ref, v_scale, kv)
        for y in range(n_y):
            at = slice(y * share, (y + 1) * share)
            for pair in range(n_pair):
                query = head(q_ref, q_scale, (kv * n_y + y) * n_pair + pair)
                rows = jnp.concatenate([query, key[at], value[at]], axis=0)
                o_ref[(y * n_kv + kv) * n_pair + pair] = rows.astype(jnp.bfloat16)


def pack(arrays, n_y, n_kv, n_pair):
    tok = arrays[0].shape[0]
    return pl.pallas_call(
        functools.partial(pack_kernel, n_y=n_y, n_kv=n_kv, n_pair=n_pair),
        out_shape=jax.ShapeDtypeStruct((n_y * n_kv * n_pair, tok + 2 * tok // n_y, HD), jnp.bfloat16),
        in_specs=[pl.BlockSpec(memory_space=pl.ANY)] * len(arrays),
        out_specs=pl.BlockSpec(memory_space=pltpu.VMEM),
        scratch_shapes=[pltpu.VMEM(a.shape, a.dtype) for a in arrays] + [pltpu.SemaphoreType.DMA((len(arrays),))],
        compiler_params=pltpu.CompilerParams(vmem_limit_bytes=60 * 2**20),
        name="pack",
    )(*arrays)


def folded(tile):
    return jnp.sum(tile.reshape(tile.shape[0] // 8, 8, tile.shape[1]), axis=0)


def sign_table():
    i = lax.broadcasted_iota(jnp.int32, (HD, HD), 0)
    j = lax.broadcasted_iota(jnp.int32, (HD, HD), 1)
    both = i & j
    odd = (both ^ (both >> 1) ^ (both >> 2) ^ (both >> 3) ^ (both >> 4)) & 1
    return jnp.where(i // HBLK == j // HBLK, 1.0 - 2.0 * odd.astype(jnp.float32), 0.0).astype(jnp.bfloat16)


def partial_kernel(order_ref, place_ref, *refs, span, groups, fresh, begun, last, edge):
    kv_count = 2 if last else 1
    kv_refs, q_ref, o_ref = refs[:kv_count], refs[kv_count], refs[kv_count + 1 + begun]
    key, value, least, most, scored, peak, acc = refs[kv_count + 2 + begun:]
    members = 2 * kv_refs[0].shape[0] // groups
    share = kv_refs[0].shape[1] // (2 * SPANS_GRP)
    per_chunk = share * QBLK // span
    key_spans = groups * SPANS_GRP
    rate = math.log2(math.e) / math.sqrt(HD)
    places = [order_ref[place_ref[n // SPANS_GRP] * SPANS_GRP + n % SPANS_GRP] for n in range(key_spans)]

    def arrange(chosen):
        for n in chosen:
            rank = sum((places[m] < places[n]).astype(jnp.int32) for m in chosen if m != n)
            at = pl.ds(pl.multiple_of(rank * span, span), span)
            for half, ref in enumerate((key, value)):
                kv_ref, group = kv_refs[n // (key_spans // 2)], n // SPANS_GRP % (groups // 2)
                start = (half * SPANS_GRP + n % SPANS_GRP) * share
                rows = kv_ref[pl.ds(group * members, members), pl.ds(start, share), :]
                ref[at, 0:HD] = rows.reshape(span, HD)

    arrange(fresh)
    value[:, HD:HD + ONES] = jnp.ones((value.shape[0], ONES), value.dtype)
    least[...] = jnp.ones_like(least)
    most[...] = jnp.ones_like(most)

    def shown(s, q_index):
        inside = lax.broadcasted_iota(jnp.int32, s.shape, 0)
        chunk = inside % share
        key_at = chunk // per_chunk * QBLK + inside // share * per_chunk + chunk % per_chunk
        return key_at <= lax.broadcasted_iota(jnp.int32, s.shape, 1) + q_index

    def write(at, summed, level):
        o_ref[0:HD, at] = (acc[0:HD, :] * (1.0 / summed)).astype(o_ref.dtype)
        row = lax.broadcasted_iota(jnp.int32, (TAIL, span), 0)
        tail = jnp.zeros((TAIL, span), jnp.float32)
        for n in range(PARTS):
            part = level.astype(jnp.bfloat16).astype(jnp.float32)
            level = level - part
            tail = jnp.where(row == n, part, tail)
        o_ref[HD:HD + TAIL, at] = tail.astype(o_ref.dtype)

    def sight(a, chosen):
        q_place = order_ref[place_ref[groups] * SPANS_GRP + a]
        count = sum((places[n] <= q_place).astype(jnp.int32) for n in chosen)
        own = functools.reduce(jnp.logical_or, [places[n] == q_place for n in chosen])
        at = pl.ds(pl.multiple_of(a * span, span), span)
        return at, count, count - own.astype(jnp.int32)

    def one(a, _):
        at, count, whole = sight(a, fresh)
        q = q_ref[at, :]
        acc[...] = refs[kv_count + 1][:, at] if begun else jnp.zeros_like(acc)

        def add(start, width, masked):
            rows = pl.ds(pl.multiple_of(start * span, span), width * span)
            s = lax.dot_general(key[rows, :], q, NT, preferred_element_type=jnp.float32) * rate
            if masked:
                s = jnp.where(shown(s, jnp.where(start < whole, span, 0)), s, NEG)
            weights = jnp.exp2(s).astype(jnp.bfloat16)
            acc[...] += lax.dot_general(value[rows, :], weights, TN, preferred_element_type=jnp.float32)

        def two(t, _):
            add(2 * t, 2, False)
            return 0

        def single(t, _):
            add(t, 1, edge)
            return 0

        pairs = lax.div(whole, 2)
        lax.fori_loop(0, pairs, two, 0)
        lax.fori_loop(2 * pairs, count, single, 0)
        if not last:
            o_ref[:, at] = acc[...]
            return 0
        summed = acc[HD:HD + 1, :]
        _, count, _ = sight(a, range(key_spans))
        summed = jnp.where(count > 0, summed, 1.0)
        least[...] = jnp.minimum(least[...], summed)
        most[...] = jnp.maximum(most[...], summed)
        write(at, summed, jnp.where(count > 0, jnp.log2(summed), NEG))
        return 0

    lax.fori_loop(0, SPANS_GRP, one, 0)
    if not last:
        return

    def again(a, _):
        at, count, whole = sight(a, range(key_spans))
        q = q_ref[at, :]
        peak[...] = jnp.full_like(peak, NEG)
        acc[...] = jnp.zeros_like(acc)

        def step(t, _):
            rows = pl.ds(pl.multiple_of(t * span, span), span)
            s = lax.dot_general(key[rows, :], q, NT, preferred_element_type=jnp.float32)
            scored[...] = jnp.where(shown(s, jnp.where(t < whole, span, 0)), s, NEG)
            old = peak[...]
            top = jnp.maximum(old, jnp.max(scored[...], axis=0, keepdims=True))
            shrink = jnp.exp2((old - top) * rate)
            weights = jnp.exp2((scored[...] - top) * rate)
            peak[...] = top
            acc[...] = acc[...] * shrink + lax.dot_general(
                value[rows, :], weights.astype(jnp.bfloat16), TN, preferred_element_type=jnp.float32
            )
            return 0

        lax.fori_loop(0, count, step, 0)
        summed = acc[HD:HD + 1, :]
        summed = jnp.where(count > 0, summed, 1.0)
        write(at, summed, jnp.where(count > 0, peak[...] * rate + jnp.log2(summed), NEG))
        return 0

    safe = (jnp.min(least[...]) > LOW) & (jnp.max(most[...]) < HIGH)

    @pl.when(jnp.logical_not(safe))
    def _():
        arrange(range(key_spans))
        lax.fori_loop(0, SPANS_GRP, again, 0)


def attend_part(order, place, query, kv, fresh, edge, dtype, begun=()):
    rows = query.shape[0]
    span = rows // SPANS_GRP
    vmem = pl.BlockSpec(memory_space=pltpu.VMEM)
    smem = pl.BlockSpec(memory_space=pltpu.SMEM)
    groups = 2 * kv[0].shape[0] * kv[0].shape[1] // (2 * rows)
    last = len(kv) == 2
    keys = (groups if last else groups // 2) * rows
    done = jax.ShapeDtypeStruct((HD + TAIL, rows), dtype)
    sums = jax.ShapeDtypeStruct((HD + ONES, rows), jnp.float32)
    return pl.pallas_call(
        functools.partial(
            partial_kernel, span=span, groups=groups, fresh=fresh, begun=len(begun), last=last, edge=edge
        ),
        out_shape=done if last else sums,
        in_specs=[smem, smem] + [vmem] * (len(kv) + 1 + len(begun)),
        out_specs=vmem,
        scratch_shapes=[
            pltpu.VMEM((keys, HD), jnp.bfloat16),
            pltpu.VMEM((keys, HD + ONES), jnp.bfloat16),
            pltpu.VMEM((1, span), jnp.float32),
            pltpu.VMEM((1, span), jnp.float32),
            pltpu.VMEM((span, span), jnp.float32),
            pltpu.VMEM((1, span), jnp.float32),
            pltpu.VMEM((HD + ONES, span), jnp.float32),
        ],
        compiler_params=pltpu.CompilerParams(vmem_limit_bytes=32 * 2**20),
        cost_estimate=pl.CostEstimate(
            flops=4 * rows * keys * HD, bytes_accessed=3 * 2**20, transcendentals=rows * keys
        ),
        name="attend_part",
    )(order, place, *kv, query, *begun)


def merge_kernel(row_ref, *refs):
    parts, o_ref, flat = refs[:-2], refs[-2], refs[-1]
    rows = o_ref.shape[0]
    levels = []
    for ref in parts:
        tail = ref[HD:HD + TAIL, :].astype(jnp.float32)
        levels.append(jnp.sum(tail, axis=0, keepdims=True))
    top = functools.reduce(jnp.maximum, levels)
    shares = [jnp.exp2(level - top) for level in levels]
    whole = 1.0 / (sum(shares) * math.sqrt(HBLK))
    out = sum(ref[0:HD, :].astype(jnp.float32) * (share * whole) for ref, share in zip(parts, shares))
    high = out.astype(jnp.bfloat16)
    low = (out - high.astype(jnp.float32)).astype(jnp.bfloat16)
    signs = sign_table()
    turned = jnp.dot(signs, high, preferred_element_type=jnp.float32)
    turned = turned + jnp.dot(signs, low, preferred_element_type=jnp.float32)
    flat[...] = turned.astype(jnp.bfloat16)
    block = math.gcd(rows, 256)
    for start in range(0, rows, block):
        want = lax.broadcasted_iota(jnp.int32, (block, rows), 0) + start
        pick = jnp.where(row_ref[...] == want, 1.0, 0.0).astype(jnp.bfloat16)
        o_ref[pl.ds(start, block), :] = lax.dot_general(
            pick, flat[...], NT, preferred_element_type=jnp.float32
        ).astype(jnp.bfloat16)


def merge(row, parts):
    rows = row.shape[1]
    vmem = pl.BlockSpec(memory_space=pltpu.VMEM)
    return pl.pallas_call(
        merge_kernel,
        out_shape=jax.ShapeDtypeStruct((rows, HD), jnp.bfloat16),
        in_specs=[vmem] * (1 + len(parts)),
        out_specs=vmem,
        scratch_shapes=[pltpu.VMEM((HD, rows), jnp.bfloat16)],
        compiler_params=pltpu.CompilerParams(vmem_limit_bytes=32 * 2**20),
        cost_estimate=pl.CostEstimate(flops=2 * rows * rows * HD, bytes_accessed=2 * 2**20, transcendentals=0),
        name="merge",
    )(row, *parts)


def per_device(q_rot, k_rot, v_rot, q_exp, k_exp, v_exp, span_order, ffn_row):
    n_xl, n_y, n_kv, n_pair = (lax.axis_size(name) for name in ("xl", "y", "kv", "pair"))
    n_x, n_core = lax.axis_size(ROW), lax.axis_size("core")
    x_at, core_at = lax.axis_index(ROW), lax.axis_index("core")
    tok = q_rot.shape[0]
    share = tok // n_y
    plane = n_y * n_kv * n_pair
    message = pack((q_rot, k_rot, v_rot, q_exp, k_exp, v_exp), n_y, n_kv, n_pair)
    got = lax.all_to_all(message, PLANE, split_axis=0, concat_axis=0, tiled=True)
    q_own = got[:, :tok].reshape(plane * tok, HD)
    piece = got[:, tok:].reshape(plane, 2, share, HD).transpose(1, 0, 2, 3).reshape(2 * plane * share, HD)

    def across(array):
        return lax.ppermute(array, ROW, [(i, n_x - 1 - i) for i in range(n_x)])

    q_far = across(q_own)
    near = n_xl * n_y
    kv = lax.all_to_all(
        jnp.broadcast_to(piece[None], (near,) + piece.shape), NEAR, split_axis=0, concat_axis=0, tiled=True
    )
    kv, q_far = lax.optimization_barrier((kv, q_far))
    kv = (kv, lax.ppermute(kv, "core", [(0, 1), (1, 0)]))
    first = lax.div(x_at, n_xl) * n_xl
    held = [(first + i) * n_core + c for c in (core_at, 1 - core_at) for i in range(n_xl)]

    def place(x):
        return jnp.stack(held + [x * n_core + core_at]).astype(jnp.int32)

    half = n_xl * SPANS_GRP
    far_place = place(n_x - 1 - x_at)
    begun = attend_part(span_order, far_place, q_far, kv[:1], range(half), False, jnp.float32)
    far = attend_part(span_order, far_place, q_far, kv, range(half, 2 * half), False, jnp.bfloat16, (begun,))
    own = attend_part(span_order, place(x_at), q_own, kv, range(2 * half), True, jnp.float32)
    results = [across(far), own]
    placed = merge(ffn_row, results)
    back = lax.all_to_all(placed.reshape(plane, tok, HD), PLANE, split_axis=0, concat_axis=0, tiled=True)
    heads = back.reshape(n_y, n_kv, n_pair, tok, HD).transpose(3, 1, 0, 2, 4)
    return heads.reshape(tok, plane * HD)


def solution(mesh):
    devices = mesh.devices.reshape(2, 2, 2, 4, 8, 2)
    axes = ("xh", "xl", "core", "y", "kv", "pair")
    inner = Mesh(devices, axes)
    rows = P(axes, None)
    return jax.shard_map(
        per_device,
        mesh=inner,
        in_specs=(rows, rows, rows, rows, rows, rows, P(), P(("xh", "xl", "core"), None)),
        out_specs=rows,
        check_vma=False,
    )
```

```python
import functools
import math

import jax
import jax.numpy as jnp
from jax import lax
from jax.experimental import pallas as pl
from jax.experimental.pallas import tpu as pltpu
from jax.sharding import Mesh, PartitionSpec as P

HD = 128
HBLK = 32
QBLK = 16
SPANS_GRP = 2
PARTS = 3
TAIL = 16
ONES = 8
LOW, HIGH = 2.0**-80, 2.0**110

NEG = -1e30
NT = (((1,), (1,)), ((), ()))
TN = (((0,), (0,)), ((), ()))
PLANE = ("y", "kv", "pair")
ROW = ("xh", "xl")
NEAR = ("xl", "y")


def factors(ref):
    width = ref.shape[1]
    blocks = HD // HBLK
    heads = width // blocks
    scale = jnp.exp2(ref[...].astype(jnp.float32))
    head = lax.broadcasted_iota(jnp.int32, (heads, width), 0)
    at = lax.broadcasted_iota(jnp.int32, (heads, width), 1)
    picked = jnp.where(at // blocks == head, scale, 0.0).astype(jnp.bfloat16)
    at = lax.broadcasted_iota(jnp.int32, (width, HD), 0)
    lane = lax.broadcasted_iota(jnp.int32, (width, HD), 1)
    spread = jnp.where(at % blocks == lane // HBLK, 1.0, 0.0).astype(jnp.bfloat16)
    return jnp.dot(picked, spread, preferred_element_type=jnp.float32)


def pack_kernel(*refs, n_y, n_kv, n_pair):
    count = 6
    sources, o_ref, held, sems = refs[:count], refs[count], refs[count + 1:2 * count + 1], refs[2 * count + 1]
    copies = [pltpu.make_async_copy(src, dst, sems.at[n]) for n, (src, dst) in enumerate(zip(sources, held))]
    for copy in copies:
        copy.start()
    for copy in copies:
        copy.wait()
    q_ref, k_ref, v_ref, qe_ref, ke_ref, ve_ref = held
    share = q_ref.shape[0] // n_y

    def head(ref, scale, n):
        return ref[:, n * HD:(n + 1) * HD].astype(jnp.float32) * scale[n:n + 1, :]

    q_scale, k_scale, v_scale = factors(qe_ref), factors(ke_ref), factors(ve_ref)
    for kv in range(n_kv):
        key, value = head(k_ref, k_scale, kv), head(v_ref, v_scale, kv)
        for y in range(n_y):
            at = slice(y * share, (y + 1) * share)
            for pair in range(n_pair):
                query = head(q_ref, q_scale, (kv * n_y + y) * n_pair + pair)
                rows = jnp.concatenate([query, key[at], value[at]], axis=0)
                o_ref[(y * n_kv + kv) * n_pair + pair] = rows.astype(jnp.bfloat16)


def pack(arrays, n_y, n_kv, n_pair):
    tok = arrays[0].shape[0]
    return pl.pallas_call(
        functools.partial(pack_kernel, n_y=n_y, n_kv=n_kv, n_pair=n_pair),
        out_shape=jax.ShapeDtypeStruct((n_y * n_kv * n_pair, tok + 2 * tok // n_y, HD), jnp.bfloat16),
        in_specs=[pl.BlockSpec(memory_space=pl.ANY)] * len(arrays),
        out_specs=pl.BlockSpec(memory_space=pltpu.VMEM),
        scratch_shapes=[pltpu.VMEM(a.shape, a.dtype) for a in arrays] + [pltpu.SemaphoreType.DMA((len(arrays),))],
        compiler_params=pltpu.CompilerParams(vmem_limit_bytes=60 * 2**20),
        name="pack",
    )(*arrays)


def folded(tile):
    return jnp.sum(tile.reshape(tile.shape[0] // 8, 8, tile.shape[1]), axis=0)


def sign_table():
    i = lax.broadcasted_iota(jnp.int32, (HD, HD), 0)
    j = lax.broadcasted_iota(jnp.int32, (HD, HD), 1)
    both = i & j
    odd = (both ^ (both >> 1) ^ (both >> 2) ^ (both >> 3) ^ (both >> 4)) & 1
    return jnp.where(i // HBLK == j // HBLK, 1.0 - 2.0 * odd.astype(jnp.float32), 0.0).astype(jnp.bfloat16)


def partial_kernel(order_ref, place_ref, *refs, span, groups, fresh, begun, last, edge):
    kv_count = 2 if last else 1
    kv_refs, q_ref, o_ref = refs[:kv_count], refs[kv_count], refs[kv_count + 1 + begun]
    key, value, least, most, scored, peak, acc = refs[kv_count + 2 + begun:]
    members = 2 * kv_refs[0].shape[0] // groups
    share = kv_refs[0].shape[1] // (2 * SPANS_GRP)
    per_chunk = share * QBLK // span
    key_spans = groups * SPANS_GRP
    rate = math.log2(math.e) / math.sqrt(HD)
    places = [order_ref[place_ref[n // SPANS_GRP] * SPANS_GRP + n % SPANS_GRP] for n in range(key_spans)]

    def arrange(chosen):
        for n in chosen:
            rank = sum((places[m] < places[n]).astype(jnp.int32) for m in chosen if m != n)
            at = pl.ds(pl.multiple_of(rank * span, span), span)
            for half, ref in enumerate((key, value)):
                kv_ref, group = kv_refs[n // (key_spans // 2)], n // SPANS_GRP % (groups // 2)
                start = (half * SPANS_GRP + n % SPANS_GRP) * share
                rows = kv_ref[pl.ds(group * members, members), pl.ds(start, share), :]
                ref[at, 0:HD] = rows.reshape(span, HD)

    arrange(fresh)
    value[:, HD:HD + ONES] = jnp.ones((value.shape[0], ONES), value.dtype)
    least[...] = jnp.ones_like(least)
    most[...] = jnp.ones_like(most)

    def shown(s, q_index):
        inside = lax.broadcasted_iota(jnp.int32, s.shape, 0)
        chunk = inside % share
        key_at = chunk // per_chunk * QBLK + inside // share * per_chunk + chunk % per_chunk
        return key_at <= lax.broadcasted_iota(jnp.int32, s.shape, 1) + q_index

    def write(at, summed, level):
        o_ref[0:HD, at] = (acc[0:HD, :] * (1.0 / summed)).astype(o_ref.dtype)
        row = lax.broadcasted_iota(jnp.int32, (TAIL, span), 0)
        tail = jnp.zeros((TAIL, span), jnp.float32)
        for n in range(PARTS):
            part = level.astype(jnp.bfloat16).astype(jnp.float32)
            level = level - part
            tail = jnp.where(row == n, part, tail)
        o_ref[HD:HD + TAIL, at] = tail.astype(o_ref.dtype)

    def sight(a, chosen):
        q_place = order_ref[place_ref[groups] * SPANS_GRP + a]
        count = sum((places[n] <= q_place).astype(jnp.int32) for n in chosen)
        own = functools.reduce(jnp.logical_or, [places[n] == q_place for n in chosen])
        at = pl.ds(pl.multiple_of(a * span, span), span)
        return at, count, count - own.astype(jnp.int32)

    def one(a, _):
        at, count, whole = sight(a, fresh)
        q = q_ref[at, :]
        acc[...] = refs[kv_count + 1][:, at] if begun else jnp.zeros_like(acc)

        def add(start, width, masked):
            rows = pl.ds(pl.multiple_of(start * span, span), width * span)
            s = lax.dot_general(key[rows, :], q, NT, preferred_element_type=jnp.float32) * rate
            if masked:
                s = jnp.where(shown(s, jnp.where(start < whole, span, 0)), s, NEG)
            weights = jnp.exp2(s).astype(jnp.bfloat16)
            acc[...] += lax.dot_general(value[rows, :], weights, TN, preferred_element_type=jnp.float32)

        def four(t, _):
            add(4 * t, 4, False)
            return 0

        def two(t, _):
            add(2 * t, 2, False)
            return 0

        def single(t, _):
            add(t, 1, edge)
            return 0

        pairs = lax.div(whole, 2)
        fours = lax.div(whole, 4)
        lax.fori_loop(0, fours, four, 0)
        lax.fori_loop(2 * fours, pairs, two, 0)
        lax.fori_loop(2 * pairs, count, single, 0)
        if not last:
            o_ref[:, at] = acc[...]
            return 0
        summed = acc[HD:HD + 1, :]
        _, count, _ = sight(a, range(key_spans))
        summed = jnp.where(count > 0, summed, 1.0)
        least[...] = jnp.minimum(least[...], summed)
        most[...] = jnp.maximum(most[...], summed)
        write(at, summed, jnp.where(count > 0, jnp.log2(summed), NEG))
        return 0

    lax.fori_loop(0, SPANS_GRP, one, 0)
    if not last:
        return

    def again(a, _):
        at, count, whole = sight(a, range(key_spans))
        q = q_ref[at, :]
        peak[...] = jnp.full_like(peak, NEG)
        acc[...] = jnp.zeros_like(acc)

        def step(t, _):
            rows = pl.ds(pl.multiple_of(t * span, span), span)
            s = lax.dot_general(key[rows, :], q, NT, preferred_element_type=jnp.float32)
            scored[...] = jnp.where(shown(s, jnp.where(t < whole, span, 0)), s, NEG)
            old = peak[...]
            top = jnp.maximum(old, jnp.max(scored[...], axis=0, keepdims=True))
            shrink = jnp.exp2((old - top) * rate)
            weights = jnp.exp2((scored[...] - top) * rate)
            peak[...] = top
            acc[...] = acc[...] * shrink + lax.dot_general(
                value[rows, :], weights.astype(jnp.bfloat16), TN, preferred_element_type=jnp.float32
            )
            return 0

        lax.fori_loop(0, count, step, 0)
        summed = acc[HD:HD + 1, :]
        summed = jnp.where(count > 0, summed, 1.0)
        write(at, summed, jnp.where(count > 0, peak[...] * rate + jnp.log2(summed), NEG))
        return 0

    safe = (jnp.min(least[...]) > LOW) & (jnp.max(most[...]) < HIGH)

    @pl.when(jnp.logical_not(safe))
    def _():
        arrange(range(key_spans))
        lax.fori_loop(0, SPANS_GRP, again, 0)


def attend_part(order, place, query, kv, fresh, edge, dtype, begun=()):
    rows = query.shape[0]
    span = rows // SPANS_GRP
    vmem = pl.BlockSpec(memory_space=pltpu.VMEM)
    smem = pl.BlockSpec(memory_space=pltpu.SMEM)
    groups = 2 * kv[0].shape[0] * kv[0].shape[1] // (2 * rows)
    last = len(kv) == 2
    keys = (groups if last else groups // 2) * rows
    done = jax.ShapeDtypeStruct((HD + TAIL, rows), dtype)
    sums = jax.ShapeDtypeStruct((HD + ONES, rows), jnp.float32)
    return pl.pallas_call(
        functools.partial(
            partial_kernel, span=span, groups=groups, fresh=fresh, begun=len(begun), last=last, edge=edge
        ),
        out_shape=done if last else sums,
        in_specs=[smem, smem] + [vmem] * (len(kv) + 1 + len(begun)),
        out_specs=vmem,
        scratch_shapes=[
            pltpu.VMEM((keys, HD), jnp.bfloat16),
            pltpu.VMEM((keys, HD + ONES), jnp.bfloat16),
            pltpu.VMEM((1, span), jnp.float32),
            pltpu.VMEM((1, span), jnp.float32),
            pltpu.VMEM((span, span), jnp.float32),
            pltpu.VMEM((1, span), jnp.float32),
            pltpu.VMEM((HD + ONES, span), jnp.float32),
        ],
        compiler_params=pltpu.CompilerParams(vmem_limit_bytes=32 * 2**20),
        cost_estimate=pl.CostEstimate(
            flops=4 * rows * keys * HD, bytes_accessed=3 * 2**20, transcendentals=rows * keys
        ),
        name="attend_part",
    )(order, place, *kv, query, *begun)


def merge_kernel(row_ref, *refs):
    parts, o_ref, flat = refs[:-2], refs[-2], refs[-1]
    rows = o_ref.shape[0]
    levels = []
    for ref in parts:
        tail = ref[HD:HD + TAIL, :].astype(jnp.float32)
        levels.append(jnp.sum(tail, axis=0, keepdims=True))
    top = functools.reduce(jnp.maximum, levels)
    shares = [jnp.exp2(level - top) for level in levels]
    whole = 1.0 / (sum(shares) * math.sqrt(HBLK))
    out = sum(ref[0:HD, :].astype(jnp.float32) * (share * whole) for ref, share in zip(parts, shares))
    high = out.astype(jnp.bfloat16)
    low = (out - high.astype(jnp.float32)).astype(jnp.bfloat16)
    signs = sign_table()
    turned = jnp.dot(signs, high, preferred_element_type=jnp.float32)
    turned = turned + jnp.dot(signs, low, preferred_element_type=jnp.float32)
    flat[...] = turned.astype(jnp.bfloat16)
    block = math.gcd(rows, 256)
    for start in range(0, rows, block):
        want = lax.broadcasted_iota(jnp.int32, (block, rows), 0) + start
        pick = jnp.where(row_ref[...] == want, 1.0, 0.0).astype(jnp.bfloat16)
        o_ref[pl.ds(start, block), :] = lax.dot_general(
            pick, flat[...], NT, preferred_element_type=jnp.float32
        ).astype(jnp.bfloat16)


def merge(row, parts):
    rows = row.shape[1]
    vmem = pl.BlockSpec(memory_space=pltpu.VMEM)
    return pl.pallas_call(
        merge_kernel,
        out_shape=jax.ShapeDtypeStruct((rows, HD), jnp.bfloat16),
        in_specs=[vmem] * (1 + len(parts)),
        out_specs=vmem,
        scratch_shapes=[pltpu.VMEM((HD, rows), jnp.bfloat16)],
        compiler_params=pltpu.CompilerParams(vmem_limit_bytes=32 * 2**20),
        cost_estimate=pl.CostEstimate(flops=2 * rows * rows * HD, bytes_accessed=2 * 2**20, transcendentals=0),
        name="merge",
    )(row, *parts)


def per_device(q_rot, k_rot, v_rot, q_exp, k_exp, v_exp, span_order, ffn_row):
    n_xl, n_y, n_kv, n_pair = (lax.axis_size(name) for name in ("xl", "y", "kv", "pair"))
    n_x, n_core = lax.axis_size(ROW), lax.axis_size("core")
    x_at, core_at = lax.axis_index(ROW), lax.axis_index("core")
    tok = q_rot.shape[0]
    share = tok // n_y
    plane = n_y * n_kv * n_pair
    message = pack((q_rot, k_rot, v_rot, q_exp, k_exp, v_exp), n_y, n_kv, n_pair)
    got = lax.all_to_all(message, PLANE, split_axis=0, concat_axis=0, tiled=True)
    q_own = got[:, :tok].reshape(plane * tok, HD)
    piece = got[:, tok:].reshape(plane, 2, share, HD).transpose(1, 0, 2, 3).reshape(2 * plane * share, HD)

    def across(array):
        return lax.ppermute(array, ROW, [(i, n_x - 1 - i) for i in range(n_x)])

    q_far = across(q_own)
    near = n_xl * n_y
    kv = lax.all_to_all(
        jnp.broadcast_to(piece[None], (near,) + piece.shape), NEAR, split_axis=0, concat_axis=0, tiled=True
    )
    kv, q_far = lax.optimization_barrier((kv, q_far))
    kv = (kv, lax.ppermute(kv, "core", [(0, 1), (1, 0)]))
    first = lax.div(x_at, n_xl) * n_xl
    held = [(first + i) * n_core + c for c in (core_at, 1 - core_at) for i in range(n_xl)]

    def place(x):
        return jnp.stack(held + [x * n_core + core_at]).astype(jnp.int32)

    half = n_xl * SPANS_GRP
    far_place = place(n_x - 1 - x_at)
    begun = attend_part(span_order, far_place, q_far, kv[:1], range(half), False, jnp.float32)
    far = attend_part(span_order, far_place, q_far, kv, range(half, 2 * half), False, jnp.bfloat16, (begun,))
    own = attend_part(span_order, place(x_at), q_own, kv, range(2 * half), True, jnp.float32)
    results = [across(far), own]
    placed = merge(ffn_row, results)
    back = lax.all_to_all(placed.reshape(plane, tok, HD), PLANE, split_axis=0, concat_axis=0, tiled=True)
    heads = back.reshape(n_y, n_kv, n_pair, tok, HD).transpose(3, 1, 0, 2, 4)
    return heads.reshape(tok, plane * HD)


def solution(mesh):
    devices = mesh.devices.reshape(2, 2, 2, 4, 8, 2)
    axes = ("xh", "xl", "core", "y", "kv", "pair")
    inner = Mesh(devices, axes)
    rows = P(axes, None)
    return jax.shard_map(
        per_device,
        mesh=inner,
        in_specs=(rows, rows, rows, rows, rows, rows, P(), P(("xh", "xl", "core"), None)),
        out_specs=rows,
        check_vma=False,
    )
```
